256 devices in a mesh: ctx: 32 (over z, y_lo, core), tp: 8 (over y_hi, x).
Axes of the slice: x: 4, y: 4 (y_hi: 2, y_lo: 2; y = y_hi * 2 + y_lo), z: 8, core: 2. Of those that a mesh axis runs over, the one named last changes fastest.
Arguments:
- hidden: bfloat16 [8192, 8192], P('ctx', 'tp'), may hold values from -6 to 6
- query_weight: bfloat16 [8192, 4096], P('ctx', 'tp')
- keys: bfloat16 [8192, 4096], P('ctx', 'tp'), may hold values from -6 to 6
- values: bfloat16 [8192, 4096], P('ctx', 'tp'), may hold values from -6 to 6
- d_attended: bfloat16 [8192, 4096], P('ctx', 'tp'), may hold values from -6 to 6
Outputs:
- attended: bfloat16 [8192, 4096], P('ctx', 'tp')
- d_hidden: bfloat16 [8192, 8192], P('ctx', 'tp')
- d_query_weight: bfloat16 [8192, 4096], P('ctx', 'tp')
- d_keys: bfloat16 [8192, 4096], P('ctx', 'tp')
- d_values: bfloat16 [8192, 4096], P('ctx', 'tp')
The draws below stay inside these ranges and needn't reach their ends.
All inputs are finite; a program needn't handle non-finite values.
Results may differ from the reference program's by a relative error of at most 0.03.
Values may be sent and summed in bfloat16 or wider, within the bound.
No kernel may reach another device: no remote copies, remote signals or barrier semaphores. Data moves between devices by JAX's collectives and lax.ppermute only.
A program may use at most 128 MiB of HBM per device.

```python
import math
import jax
import jax.numpy as jnp
from jax import lax

D = 8192
DH = 128
W = 512
SEQ_DEVS = 16
TOK_DEV = 256
HD = 4096
TOKENS = 8192
N_TP = 8


def draw_hidden(key, part):
    key = jax.random.fold_in(key, 11)
    result = jax.random.truncated_normal(key, -6.0, 6.0, (TOKENS, D), jnp.float32)
    return result.astype(jnp.bfloat16)


def draw_query_weight(key, part):
    key = jax.random.fold_in(key, 23)
    base = jax.random.truncated_normal(key, -5.0, 5.0, (D, HD), jnp.float32) * (1.0 / math.sqrt(D))
    result = base
    return result.astype(jnp.bfloat16)


def draw_keys(key, part):
    key = jax.random.fold_in(key, 37)
    result = jax.random.truncated_normal(key, -6.0, 6.0, (TOKENS, HD), jnp.float32)
    return result.astype(jnp.bfloat16)


def steps_of(own_key, shape, pieces, low, top_value):
    factor_of = 1.0
    for dim, blocks in pieces:
        draws = jax.random.uniform(jax.random.fold_in(jax.random.fold_in(own_key, 6), dim), (blocks,), jnp.float32, low / len(pieces), top_value / len(pieces))
        factor_of = factor_of * jnp.repeat(jnp.exp(draws), shape[dim] // blocks).reshape((-1,) + (1,) * (len(shape) - 1 - dim))
    return factor_of


def noise(key, shape, deviation, most, cuts=(), held_as=jnp.bfloat16):
    loudness = steps_of(key, shape, cuts, -0.22, 0.18) if cuts else 1.0
    drawn = jax.random.normal(key, shape, jnp.float32) * deviation * loudness
    return jnp.minimum(jnp.maximum(drawn, -most), most).astype(held_as)


def setup_inputs(seed: int = 0) -> dict:
    splits = jax.random.split(jax.random.key(seed), 6)
    return {
        "hidden": draw_hidden(jax.random.fold_in(splits[5], 71), 0),
        "query_weight": draw_query_weight(jax.random.fold_in(splits[5], 71), 0),
        "keys": draw_keys(jax.random.fold_in(splits[5], 71), 0),
        "values": noise(splits[3], (TOKENS, HD), 1.0, 6.0, ((0, 32), (1, 8))),
        "d_attended": noise(splits[4], (TOKENS, HD), 1.0, 6.0, ((0, 32), (1, 8))),
    }


def attend(query, keys, values, d_out, visible):
    rows = query.shape[0]
    krows = keys.shape[0]
    heads = query.shape[1] // DH
    scale = 1.0 / (DH ** 0.5)
    qh = query.reshape(rows, heads, DH)
    kh = keys.reshape(krows, heads, DH)
    vh = values.reshape(krows, heads, DH)
    dh_out = d_out.reshape(rows, heads, DH)
    scores = jnp.einsum("qhd,khd->hqk", qh, kh, preferred_element_type=jnp.float32) * scale
    scores = jnp.where(visible[None], scores, -1e30)
    top = jnp.max(scores, axis=-1, keepdims=True)
    expo = jnp.where(visible[None], jnp.exp(scores - top), 0.0)
    prob = expo / jnp.sum(expo, axis=-1, keepdims=True)
    prob_b = prob.astype(jnp.bfloat16)
    output = jnp.einsum("hqk,khd->qhd", prob_b, vh, preferred_element_type=jnp.float32).astype(jnp.bfloat16)
    dprob = jnp.einsum("qhd,khd->hqk", dh_out, vh, preferred_element_type=jnp.float32)
    delta = jnp.sum(prob * dprob, axis=-1, keepdims=True)
    dscore = (prob * (dprob - delta) * scale).astype(jnp.bfloat16)
    d_query = jnp.einsum("hqk,khd->qhd", dscore, kh, preferred_element_type=jnp.float32).astype(jnp.bfloat16)
    d_keys = jnp.einsum("hqk,qhd->khd", dscore, qh, preferred_element_type=jnp.float32)
    d_values = jnp.einsum("hqk,qhd->khd", prob_b, dh_out, preferred_element_type=jnp.float32)
    width = heads * DH
    return (output.reshape(rows, width), d_query.reshape(rows, width),
            d_keys.reshape(krows, width), d_values.reshape(krows, width))


def reference(hidden, query_weight, keys, values, d_attended):
    query = jnp.dot(hidden, query_weight, preferred_element_type=jnp.float32).astype(jnp.bfloat16)
    tokens = hidden.shape[0]
    width = query.shape[1]
    seq_len = TOK_DEV * SEQ_DEVS
    blocks = tokens // TOK_DEV
    keys_pad = jnp.pad(keys, ((W, 0), (0, 0)))
    values_pad = jnp.pad(values, ((W, 0), (0, 0)))

    def step(carry, index):
        dk_pad, dv_pad = carry
        start = (index * TOK_DEV).astype(jnp.int32)
        q_rows = lax.dynamic_slice_in_dim(query, start, TOK_DEV, 0)
        g_rows = lax.dynamic_slice_in_dim(d_attended, start, TOK_DEV, 0)
        k_rows = lax.dynamic_slice_in_dim(keys_pad, start, TOK_DEV + W, 0)
        v_rows = lax.dynamic_slice_in_dim(values_pad, start, TOK_DEV + W, 0)
        qpos = start + jnp.arange(TOK_DEV, dtype=jnp.int32)
        kpos = start - W + jnp.arange(TOK_DEV + W, dtype=jnp.int32)
        differ = qpos[:, None] - kpos[None, :]
        visible = (kpos[None, :] >= 0) & (qpos[:, None] // seq_len == kpos[None, :] // seq_len) & (differ >= 0) & (differ < W)
        output, d_query, d_k, d_v = attend(q_rows, k_rows, v_rows, g_rows, visible)
        dk_pad = lax.dynamic_update_slice_in_dim(dk_pad, lax.dynamic_slice_in_dim(dk_pad, start, TOK_DEV + W, 0) + d_k, start, 0)
        dv_pad = lax.dynamic_update_slice_in_dim(dv_pad, lax.dynamic_slice_in_dim(dv_pad, start, TOK_DEV + W, 0) + d_v, start, 0)
        return (dk_pad, dv_pad), (output, d_query)

    zeros = jnp.zeros((tokens + W, width), jnp.float32)
    (dk_pad, dv_pad), (outputs, d_queries) = lax.scan(step, (zeros, zeros), jnp.arange(blocks, dtype=jnp.int32))
    attended = outputs.reshape(tokens, width)
    d_query = d_queries.reshape(tokens, width)
    d_keys = dk_pad[W:].astype(jnp.bfloat16)
    d_values = dv_pad[W:].astype(jnp.bfloat16)
    block_width = width // N_TP
    total = jnp.zeros(hidden.shape, jnp.float32)
    for block in range(N_TP):
        low = block * block_width
        part = jnp.dot(d_query[:, low:low + block_width], query_weight[:, low:low + block_width].T, preferred_element_type=jnp.float32)
        total = total + part.astype(jnp.bfloat16).astype(jnp.float32)
    d_hidden = total.astype(jnp.bfloat16)
    d_query_weight = jnp.dot(hidden.T, d_query, preferred_element_type=jnp.float32).astype(jnp.bfloat16)
    return attended, d_hidden, d_query_weight, d_keys, d_values
```

```python
import jax
import jax.numpy as jnp
from jax import lax
from jax.experimental import pallas as pl
from jax.experimental.pallas import tpu as pltpu
from jax.sharding import Mesh, PartitionSpec as P

DH = 128
W = 512
SEQ_Z = 4
AXES = ("z", "yl", "co", "yh", "x")
SIZES = (8, 2, 2, 2, 4)
NZ, NX = 8, 4
T = 256
SCALE = 1.0 / DH**0.5
LOG2E = 1.4426950408889634
BF = jnp.bfloat16
F32 = jnp.float32
VMEM = 56 * 1024 * 1024


def route(target):
    pairs = []
    for i in range(256):
        rest, place = i, []
        for size in SIZES[::-1]:
            place.append(rest % size)
            rest //= size
        there = target(*place[::-1])
        j = 0
        for size, c in zip(SIZES, there):
            j = j * size + c % size
        pairs.append((i, j))
    return pairs


def move(block, dz=0, yl=0, co=0, yh=0, dx=0):
    pairs = route(lambda z, a, b, c, x: (z + dz, a ^ yl, b ^ co, c ^ yh, x + dx))
    return lax.ppermute(block, AXES, pairs)


def params():
    return pltpu.CompilerParams(vmem_limit_bytes=VMEM)


def cost(flops, bytes_accessed, exps=0):
    return pl.CostEstimate(flops=flops, bytes_accessed=bytes_accessed, transcendentals=exps)


def mm(a, b, dims):
    return lax.dot_general(a, b, (dims, ((), ())), preferred_element_type=F32)


def query_kernel(place_ref, own_ref, other_ref, wa_ref, wb_ref, out_ref, acc_ref):
    step = pl.program_id(0)

    @pl.when(step == 0)
    def _():
        acc_ref[...] = jnp.zeros_like(acc_ref)

    for dc, ref in enumerate((own_ref, other_ref)):
        h = ref[0].reshape(2 * T, T)
        acc_ref[dc, :, : 2 * DH] += mm(h, wa_ref[0], ((1,), (0,)))
        acc_ref[dc, :, 2 * DH :] += mm(h, wb_ref[0], ((1,), (0,)))

    @pl.when(step == 7)
    def _():
        for dc in range(2):
            for dl in range(2):
                row = pl.multiple_of(place_ref[8 + dc * 2 + dl] * T, T)
                for k in range(4):
                    out_ref[k, pl.ds(row, T), :] = acc_ref[
                        dc, dl * T : (dl + 1) * T, k * DH : (k + 1) * DH
                    ].astype(BF)


def query_part(place, own, other, wa, wb):
    block = pl.BlockSpec((1, 2, T, T), lambda i, p: (i, 0, 0, 0))
    wblock = pl.BlockSpec((1, T, 2 * DH), lambda i, p: (p[i], 0, 0))
    return pl.pallas_call(
        query_kernel,
        grid_spec=pltpu.PrefetchScalarGridSpec(
            num_scalar_prefetch=1,
            grid=(8,),
            in_specs=[block, block, wblock, wblock],
            out_specs=pl.BlockSpec((4, 4 * T, DH), lambda i, p: (0, 0, 0)),
            scratch_shapes=[pltpu.VMEM((2, 2 * T, 4 * DH), F32)],
        ),
        out_shape=jax.ShapeDtypeStruct((4, 4 * T, DH), BF),
        compiler_params=params(),
        cost_estimate=cost(2 * 1024 * 2048 * 512, 7 << 20),
        name="query_part",
    )(place, own, other, wa, wb)


def d_hidden_kernel(place_ref, dq_ref, wa_ref, wb_ref, out_ref):
    for dl in range(2):
        row = pl.multiple_of(place_ref[8 + dl] * T, T)
        part = mm(dq_ref[0, pl.ds(row, T), :], wa_ref[0, :, :DH], ((1,), (1,)))
        part += mm(dq_ref[1, pl.ds(row, T), :], wa_ref[0, :, DH:], ((1,), (1,)))
        part += mm(dq_ref[2, pl.ds(row, T), :], wb_ref[0, :, :DH], ((1,), (1,)))
        part += mm(dq_ref[3, pl.ds(row, T), :], wb_ref[0, :, DH:], ((1,), (1,)))
        out_ref[0, dl] = part.astype(BF)


def d_hidden_part(place, dq, wa, wb):
    wblock = pl.BlockSpec((1, T, 2 * DH), lambda i, p: (p[i], 0, 0))
    return pl.pallas_call(
        d_hidden_kernel,
        grid_spec=pltpu.PrefetchScalarGridSpec(
            num_scalar_prefetch=1,
            grid=(8,),
            in_specs=[pl.BlockSpec((4, 4 * T, DH), lambda i, p: (0, 0, 0)), wblock, wblock],
            out_specs=pl.BlockSpec((1, 2, T, T), lambda i, p: (i, 0, 0, 0)),
        ),
        out_shape=jax.ShapeDtypeStruct((8, 2, T, T), BF),
        compiler_params=params(),
        cost_estimate=cost(1024 * 2048 * 512, 5 << 20),
        name="d_hidden_part",
    )(place, dq, wa, wb)


def d_weight_kernel(place_ref, own_ref, other_ref, dq_ref, outa_ref, outb_ref):
    for half, out_ref in enumerate((outa_ref, outb_ref)):
        for k in range(2):
            total = jnp.zeros((T, DH), F32)
            for dc, ref in enumerate((own_ref, other_ref)):
                for dl in range(2):
                    row = pl.multiple_of(place_ref[8 + dc * 2 + dl] * T, T)
                    total += mm(
                        ref[0, dl], dq_ref[half * 2 + k, pl.ds(row, T), :], ((0,), (0,))
                    )
            out_ref[0, :, k * DH : (k + 1) * DH] = total.astype(BF)


def d_weight_part(place, own, other, dq):
    block = pl.BlockSpec((1, 2, T, T), lambda i, p: (i, 0, 0, 0))
    wblock = pl.BlockSpec((1, T, 2 * DH), lambda i, p: (p[i], 0, 0))
    return pl.pallas_call(
        d_weight_kernel,
        grid_spec=pltpu.PrefetchScalarGridSpec(
            num_scalar_prefetch=1,
            grid=(8,),
            in_specs=[block, block, pl.BlockSpec((4, 4 * T, DH), lambda i, p: (0, 0, 0))],
            out_specs=[wblock, wblock],
        ),
        out_shape=[jax.ShapeDtypeStruct((8, T, 2 * DH), BF)] * 2,
        compiler_params=params(),
        cost_estimate=cost(2 * 1024 * 2048 * 512, 7 << 20),
        name="d_weight_part",
    )(place, own, other, dq)


def attend_kernel(
    first_ref, q0_ref, q1_ref, q2_ref, q3_ref, kvd_ref, prev_ref,
    out_ref, dq_ref, dkv_ref, dprev_ref, k_ref, v_ref, dk_ref, dv_ref,
):
    k_ref[:W] = prev_ref[0]
    v_ref[:W] = prev_ref[1]
    k_ref[W:] = kvd_ref[0]
    v_ref[W:] = kvd_ref[1]
    dk_ref[...] = jnp.zeros_like(dk_ref)
    dv_ref[...] = jnp.zeros_like(dv_ref)
    inside = first_ref[0] == 0
    rows = lax.broadcasted_iota(jnp.int32, (T, T), 0)
    cols = lax.broadcasted_iota(jnp.int32, (T, T), 1)
    old = cols > rows
    for i in range(4):
        at = slice(i * T, (i + 1) * T)
        window = slice(i * T, i * T + W + T)
        q = (
            q0_ref[at].astype(F32) + q1_ref[at].astype(F32)
            + q2_ref[at].astype(F32) + q3_ref[at].astype(F32)
        ).astype(BF)
        g = kvd_ref[2, at]
        k = k_ref[window]
        v = v_ref[window]
        s = mm(q, k, ((1,), (1,)))
        sa, sb, sc = s[:, :T], s[:, T : 2 * T], s[:, 2 * T :]
        if i < 2:
            sa = jnp.where(inside, sa, -1e30)
        if i < 1:
            sb = jnp.where(inside, sb, -1e30)
        sm = jnp.where(old, sa, sc)
        top = jnp.max(jnp.maximum(sm, sb), axis=1, keepdims=True)
        em = jnp.exp2((sm - top) * (SCALE * LOG2E))
        eb = jnp.exp2((sb - top) * (SCALE * LOG2E))
        inv = 1.0 / jnp.sum(em + eb, axis=1, keepdims=True)
        pm = em * inv
        pb = eb * inv
        prob = jnp.concatenate(
            [
                jnp.where(old, pm, 0.0).astype(BF),
                pb.astype(BF),
                jnp.where(old, 0.0, pm).astype(BF),
            ],
            axis=1,
        )
        out_ref[at] = mm(prob, v, ((1,), (0,))).astype(BF)
        dp = mm(g, v, ((1,), (1,)))
        dpm = jnp.where(old, dp[:, :T], dp[:, 2 * T :])
        dpb = dp[:, T : 2 * T]
        delta = jnp.sum(pm * dpm + pb * dpb, axis=1, keepdims=True)
        dsm = pm * (dpm - delta) * SCALE
        dsb = pb * (dpb - delta) * SCALE
        ds = jnp.concatenate(
            [
                jnp.where(old, dsm, 0.0).astype(BF),
                dsb.astype(BF),
                jnp.where(old, 0.0, dsm).astype(BF),
            ],
            axis=1,
        )
        dq_ref[at] = mm(ds, k, ((1,), (0,))).astype(BF)
        dk_ref[window] += mm(ds, q, ((0,), (0,)))
        dv_ref[window] += mm(prob, g, ((0,), (0,)))
    dprev_ref[0] = dk_ref[:W].astype(BF)
    dprev_ref[1] = dv_ref[:W].astype(BF)
    dkv_ref[0] = dk_ref[W:]
    dkv_ref[1] = dv_ref[W:]


def attend(first, parts, kvd, prev):
    vm = pl.BlockSpec(memory_space=pltpu.VMEM)
    n = 4 * T
    return pl.pallas_call(
        attend_kernel,
        in_specs=[pl.BlockSpec(memory_space=pltpu.SMEM)] + [vm] * 6,
        out_specs=[vm] * 4,
        out_shape=[
            jax.ShapeDtypeStruct((n, DH), BF),
            jax.ShapeDtypeStruct((n, DH), BF),
            jax.ShapeDtypeStruct((2, n, DH), F32),
            jax.ShapeDtypeStruct((2, W, DH), BF),
        ],
        scratch_shapes=[
            pltpu.VMEM((W + n, DH), BF),
            pltpu.VMEM((W + n, DH), BF),
            pltpu.VMEM((W + n, DH), F32),
            pltpu.VMEM((W + n, DH), F32),
        ],
        compiler_params=params(),
        cost_estimate=cost(12 * n * 768 * DH, 5 << 20, n * W),
        name="attend",
    )(first, *parts, kvd, prev)


def put(buffer, block, index):
    return lax.dynamic_update_index_in_dim(buffer, block, index, 0)


def ring_gather(shard, z, ups, downs):
    buffer = put(jnp.zeros((NZ,) + shard.shape, shard.dtype), shard, z)
    up = down = shard
    for d in range(1, 5):
        if d <= ups:
            up = move(up, dz=1)
            buffer = put(buffer, up, (z - d) % NZ)
        if d <= downs:
            down = move(down, dz=-1)
            buffer = put(buffer, down, (z + d) % NZ)
    return buffer


def ring_sum(blocks, z, ups, downs):
    def part(d):
        return lax.dynamic_index_in_dim(blocks, (z + d) % NZ, 0, keepdims=False)

    up, down = part(ups), part(-downs)
    for d in range(4, 0, -1):
        if d <= ups:
            up = move(up, dz=1)
            if d > 1:
                up = (up.astype(F32) + part(d - 1).astype(F32)).astype(BF)
        if d <= downs:
            down = move(down, dz=-1)
            if d > 1:
                down = (down.astype(F32) + part(1 - d).astype(F32)).astype(BF)
    return up.astype(F32) + down.astype(F32) + part(0).astype(F32)


def per_device(hidden, weight, keys, values, d_attended):
    z, yl, co, yh, x = (lax.axis_index(a) for a in AXES)
    steps = [(dx, dy) for dx in range(NX) for dy in range(2)]
    blocks = [(yh ^ dy) * NX + (x - dx) % NX for dx, dy in steps]
    rows = [(yl ^ dl) * 2 + (co ^ dc) for dc in range(2) for dl in range(2)]
    place = jnp.stack(blocks + rows).astype(jnp.int32)
    place_other = jnp.stack(blocks + rows[2:]).astype(jnp.int32)

    def weight_piece(dc, dy):
        half = lax.dynamic_slice_in_dim(weight, (yh ^ dy) * DH, DH, 0)
        return jnp.concatenate(
            [
                lax.dynamic_slice_in_dim(half, ((yl ^ dl) * 2 + (co ^ dc)) * DH, DH, 1)
                for dl in range(2)
            ],
            axis=1,
        )

    def weight_shard(dy):
        mine = weight_piece(0, dy)
        theirs = weight_piece(1, dy)
        if dy:
            mine = move(mine, yh=1)
            theirs = move(theirs, yh=1, co=1)
        else:
            theirs = move(theirs, co=1)
        return jnp.where(
            co == 0,
            jnp.concatenate([mine, theirs], axis=0),
            jnp.concatenate([theirs, mine], axis=0),
        )

    wa = ring_gather(weight_shard(0), z, 4, 3)
    wb = ring_gather(weight_shard(1), z, 3, 4)

    def hidden_piece(dy, dl):
        part = lax.dynamic_slice_in_dim(hidden, (yl ^ dl) * 2 * T, 2 * T, 1)
        part = part.reshape(T, 2, 2, DH)
        return lax.dynamic_index_in_dim(part, yh ^ dy, 2, keepdims=False).reshape(T, T)

    mixed = []
    for dy in range(2):
        for dl in range(2):
            piece = hidden_piece(dy, dl)
            mixed.append(move(piece, yl=dl, yh=dy) if dl or dy else piece)
    mixed = jnp.stack(mixed).reshape(2, 2, T, T)
    own = jnp.stack([move(mixed, dx=dx) if dx else mixed for dx in range(NX)])
    own = own.reshape(8, 2, T, T)
    other = move(own, co=1)

    kvd = jnp.zeros((4, 3, T, DH), BF)
    for dl in range(2):
        for dc in range(2):
            at = (yl ^ dl) * 2 + (co ^ dc)
            piece = jnp.stack(
                [
                    lax.dynamic_slice_in_dim(a, at * DH, DH, 1)
                    for a in (keys, values, d_attended)
                ]
            )
            piece = move(piece, yl=dl, co=dc) if dl or dc else piece
            kvd = put(kvd, piece, at)
    kvd = kvd.transpose(1, 0, 2, 3).reshape(3, 4 * T, DH)
    prev = move(kvd[:2, W:], dz=1)

    parts = query_part(place, own, other, wa, wb)
    parts = [parts[0]] + [move(parts[k], yh=k // 2, yl=k % 2) for k in range(1, 4)]
    first = (z % SEQ_Z == 0).astype(jnp.int32).reshape(1)
    attended, dq, dkv, dprev = attend(first, parts, kvd, prev)

    dq = jnp.stack([dq] + [move(dq, yh=k // 2, yl=k % 2) for k in range(1, 4)])

    dwa, dwb = d_weight_part(place, own, other, dq)
    away = move(d_hidden_part(place_other, dq, wa, wb), co=1)
    near = d_hidden_part(place, dq, wa, wb)

    def weight_back(shard, dy):
        mine = lax.dynamic_slice_in_dim(shard, co * DH, DH, 0)
        theirs = lax.dynamic_slice_in_dim(shard, (1 - co) * DH, DH, 0)
        if dy:
            return move(mine, yh=1), move(theirs, yh=1, co=1)
        return mine, move(theirs, co=1)

    back = [
        weight_back(ring_sum(dwa, z, 4, 3).astype(BF), 0),
        weight_back(ring_sum(dwb, z, 3, 4).astype(BF), 1),
    ]
    d_weight = jnp.zeros((2, 4, DH, DH), BF)
    for dy in range(2):
        for dc in range(2):
            for dl in range(2):
                block = back[dy][dc][:, dl * DH : (dl + 1) * DH]
                d_weight = lax.dynamic_update_slice(
                    d_weight, block[None, None], (yh ^ dy, (yl ^ dl) * 2 + (co ^ dc), 0, 0)
                )
    d_weight = d_weight.transpose(0, 2, 1, 3).reshape(T, 4 * DH)

    total = near.astype(F32) + away.astype(F32)
    total = total.astype(BF).reshape(NX, 2, 2, T, T)
    line = total[0].astype(F32)
    for dx in range(1, NX):
        line = line + move(total[dx], dx=-dx).astype(F32)
    line = line.astype(BF)
    d_hidden = jnp.zeros((2, 2, T, T), BF)
    for dy in range(2):
        for dl in range(2):
            piece = line[dy, dl]
            piece = move(piece, yl=dl, yh=dy) if dl or dy else piece
            d_hidden = lax.dynamic_update_slice(
                d_hidden, piece[None, None], (yl ^ dl, yh ^ dy, 0, 0)
            )
    d_hidden = d_hidden.reshape(2, 2, T, 2, DH).transpose(2, 0, 3, 1, 4).reshape(T, 8 * DH)

    late = move(dprev, dz=-1)
    dkv = jnp.concatenate([dkv[:, :W], dkv[:, W:] + late.astype(F32)], axis=1).astype(BF)
    outs = jnp.concatenate([attended[None], dkv], axis=0).reshape(3, 4, T, DH)
    result = jnp.zeros((4, 3, T, DH), BF)
    for dl in range(2):
        for dc in range(2):
            at = (yl ^ dl) * 2 + (co ^ dc)
            piece = lax.dynamic_index_in_dim(outs, at, 1, keepdims=False)
            piece = move(piece, yl=dl, co=dc) if dl or dc else piece
            result = put(result, piece, at)
    result = result.transpose(1, 2, 0, 3).reshape(3, T, 4 * DH)
    return result[0], d_hidden, d_weight, result[1], result[2]


def solution(mesh):
    grid = Mesh(mesh.devices.reshape(SIZES), AXES)
    spec = P(("z", "yl", "co"), ("yh", "x"))
    return jax.shard_map(
        per_device, mesh=grid, in_specs=(spec,) * 5, out_specs=(spec,) * 5, check_vma=False
    )
```

```python
import jax
import jax.numpy as jnp
from jax import lax
from jax.experimental import pallas as pl
from jax.experimental.pallas import tpu as pltpu
from jax.sharding import Mesh, PartitionSpec as P

DH = 128
W = 512
SEQ_Z = 4
AXES = ("z", "yl", "co", "yh", "x")
SIZES = (8, 2, 2, 2, 4)
NZ, NX = 8, 4
T = 256
SCALE = 1.0 / DH**0.5
LOG2E = 1.4426950408889634
BF = jnp.bfloat16
F32 = jnp.float32
VMEM = 56 * 1024 * 1024


def route(target):
    pairs = []
    for i in range(256):
        rest, place = i, []
        for size in SIZES[::-1]:
            place.append(rest % size)
            rest //= size
        there = target(*place[::-1])
        j = 0
        for size, c in zip(SIZES, there):
            j = j * size + c % size
        pairs.append((i, j))
    return pairs


def move(block, dz=0, yl=0, co=0, yh=0, dx=0):
    pairs = route(lambda z, a, b, c, x: (z + dz, a ^ yl, b ^ co, c ^ yh, x + dx))
    return lax.ppermute(block, AXES, pairs)


def params():
    return pltpu.CompilerParams(vmem_limit_bytes=VMEM)


def cost(flops, bytes_accessed, exps=0):
    return pl.CostEstimate(flops=flops, bytes_accessed=bytes_accessed, transcendentals=exps)


def mm(a, b, dims):
    return lax.dot_general(a, b, (dims, ((), ())), preferred_element_type=F32)


def query_kernel(place_ref, own_ref, other_ref, *refs):
    out_ref = refs[8]
    w = jnp.concatenate([refs[r][...] for r in range(8)], axis=0)
    for dc, ref in enumerate((own_ref, other_ref)):
        for dl in range(2):
            h = jnp.concatenate([ref[place_ref[r], dl] for r in range(8)], axis=1)
            part = mm(h, w, ((1,), (0,))).astype(BF)
            row = pl.multiple_of(place_ref[8 + dc * 2 + dl] * T, T)
            for k in range(4):
                out_ref[k, pl.ds(row, T), :] = part[:, k * DH : (k + 1) * DH]


def in_vmem(kernel, name, work, outs, *args):
    vm = pl.BlockSpec(memory_space=pltpu.VMEM)
    return pl.pallas_call(
        kernel,
        in_specs=[pl.BlockSpec(memory_space=pltpu.SMEM)] + [vm] * (len(args) - 1),
        out_specs=[vm] * len(outs),
        out_shape=[jax.ShapeDtypeStruct(shape, kind) for shape, kind in outs],
        compiler_params=params(),
        cost_estimate=work,
        name=name,
    )(*args)


def query_part(place, own, other, weights):
    work = cost(2 * 1024 * 2048 * 512, 7 << 20)
    return in_vmem(
        query_kernel, "query_part", work, [((4, 4 * T, DH), BF)], place, own, other, *weights
    )[0]


def d_hidden_kernel(place_ref, *refs):
    out_ref = refs[12]
    for dl in range(2):
        row = pl.multiple_of(place_ref[8 + dl] * T, T)
        dq = jnp.concatenate([refs[k][pl.ds(row, T), :] for k in range(4)], axis=1)
        for r in range(8):
            out_ref[place_ref[r], dl] = mm(dq, refs[4 + r][...], ((1,), (1,))).astype(BF)


def d_hidden_part(place, dq, weights):
    work = cost(1024 * 2048 * 512, 5 << 20)
    return in_vmem(
        d_hidden_kernel, "d_hidden_part", work, [((8, 2, T, T), BF)], place, *dq, *weights
    )[0]


def d_weight_kernel(place_ref, own_ref, other_ref, *refs):
    dq = jnp.concatenate(
        [
            jnp.concatenate(
                [
                    refs[k][pl.ds(pl.multiple_of(place_ref[8 + j] * T, T), T), :]
                    for k in range(4)
                ],
                axis=1,
            )
            for j in range(4)
        ],
        axis=0,
    )
    for r in range(8):
        i = place_ref[r]
        h = jnp.concatenate(
            [own_ref[i, 0], own_ref[i, 1], other_ref[i, 0], other_ref[i, 1]], axis=0
        )
        refs[4 + r][...] = mm(h, dq, ((0,), (0,))).astype(BF)


def d_weight_part(place, own, other, dq):
    work = cost(2 * 1024 * 2048 * 512, 7 << 20)
    return in_vmem(
        d_weight_kernel, "d_weight_part", work, [((T, 4 * DH), BF)] * 8, place, own, other, *dq
    )


def attended_kernel(place_ref, *refs):
    for k in range(4):
        at = pl.multiple_of(place_ref[12 + k] * DH, DH)
        for j in range(3):
            refs[4 + j][:, pl.ds(at, DH)] = refs[k][j]


def d_hidden_kernel_last(place_ref, *refs):
    for k in range(4):
        at = place_ref[16 + k]
        for co in range(2):
            first = pl.multiple_of((at + co * 2) * DH, DH)
            refs[4][:, pl.ds(first, DH)] = refs[k][:, co * DH : (co + 1) * DH]


def d_weight_kernel_last(place_ref, *refs):
    for dy in range(2):
        row = pl.multiple_of(place_ref[20 + dy] * DH, DH)
        for dc in range(2):
            for dl in range(2):
                at = pl.multiple_of(place_ref[12 + dl * 2 + dc] * DH, DH)
                refs[4][pl.ds(row, DH), pl.ds(at, DH)] = refs[dy * 2 + dc][
                    :, dl * DH : (dl + 1) * DH
                ]


def attend_kernel(
    place_ref, q0_ref, q1_ref, q2_ref, q3_ref, p0_ref, p1_ref, p2_ref, p3_ref, prev_ref,
    out_ref, dq_ref, dkv_ref, dprev_ref, k_ref, v_ref, g_ref, o_ref, dk_ref, dv_ref,
):
    tokens = [pl.multiple_of(place_ref[12 + k] * T, T) for k in range(4)]
    for half in range(2):
        k_ref[half * T : (half + 1) * T] = prev_ref[half, 0]
        v_ref[half * T : (half + 1) * T] = prev_ref[half, 1]
    for row, ref in zip(tokens, (p0_ref, p1_ref, p2_ref, p3_ref)):
        k_ref[pl.ds(W + row, T), :] = ref[0]
        v_ref[pl.ds(W + row, T), :] = ref[1]
        g_ref[pl.ds(row, T), :] = ref[2]
    dk_ref[...] = jnp.zeros_like(dk_ref)
    dv_ref[...] = jnp.zeros_like(dv_ref)
    inside = place_ref[22] == 0
    rows = lax.broadcasted_iota(jnp.int32, (T, T), 0)
    cols = lax.broadcasted_iota(jnp.int32, (T, T), 1)
    old = cols > rows
    for i in range(4):
        at = slice(i * T, (i + 1) * T)
        window = slice(i * T, i * T + W + T)
        q = (
            q0_ref[at].astype(F32) + q1_ref[at].astype(F32)
            + q2_ref[at].astype(F32) + q3_ref[at].astype(F32)
        ).astype(BF)
        g = g_ref[at]
        k = k_ref[window]
        v = v_ref[window]
        s = mm(q, k, ((1,), (1,)))
        sa, sb, sc = s[:, :T], s[:, T : 2 * T], s[:, 2 * T :]
        if i < 2:
            sa = jnp.where(inside, sa, -1e30)
        if i < 1:
            sb = jnp.where(inside, sb, -1e30)
        sm = jnp.where(old, sa, sc)
        top = jnp.max(jnp.maximum(sm, sb), axis=1, keepdims=True)
        em = jnp.exp2((sm - top) * (SCALE * LOG2E))
        eb = jnp.exp2((sb - top) * (SCALE * LOG2E))
        inv = 1.0 / jnp.sum(em + eb, axis=1, keepdims=True)
        pm = em * inv
        pb = eb * inv
        prob = jnp.concatenate(
            [
                jnp.where(old, pm, 0.0).astype(BF),
                pb.astype(BF),
                jnp.where(old, 0.0, pm).astype(BF),
            ],
            axis=1,
        )
        o_ref[at] = mm(prob, v, ((1,), (0,))).astype(BF)
        dp = mm(g, v, ((1,), (1,)))
        dpm = jnp.where(old, dp[:, :T], dp[:, 2 * T :])
        dpb = dp[:, T : 2 * T]
        delta = jnp.sum(pm * dpm + pb * dpb, axis=1, keepdims=True)
        dsm = pm * (dpm - delta) * SCALE
        dsb = pb * (dpb - delta) * SCALE
        ds = jnp.concatenate(
            [
                jnp.where(old, dsm, 0.0).astype(BF),
                dsb.astype(BF),
                jnp.where(old, 0.0, dsm).astype(BF),
            ],
            axis=1,
        )
        dq_ref[at] = mm(ds, k, ((1,), (0,))).astype(BF)
        dk_ref[window] += mm(ds, q, ((0,), (0,)))
        dv_ref[window] += mm(prob, g, ((0,), (0,)))
    for half in range(2):
        dprev_ref[half, 0] = dk_ref[half * T : (half + 1) * T].astype(BF)
        dprev_ref[half, 1] = dv_ref[half * T : (half + 1) * T].astype(BF)
    for k, row in enumerate(tokens):
        out_ref[k] = o_ref[pl.ds(row, T), :]
        dkv_ref[k, 0] = dk_ref[pl.ds(W + row, T), :]
        dkv_ref[k, 1] = dv_ref[pl.ds(W + row, T), :]


def attend(place, parts, pieces, prev):
    vm = pl.BlockSpec(memory_space=pltpu.VMEM)
    n = 4 * T
    return pl.pallas_call(
        attend_kernel,
        in_specs=[pl.BlockSpec(memory_space=pltpu.SMEM)] + [vm] * 9,
        out_specs=[vm] * 4,
        out_shape=[
            jax.ShapeDtypeStruct((4, T, DH), BF),
            jax.ShapeDtypeStruct((n, DH), BF),
            jax.ShapeDtypeStruct((4, 2, T, DH), F32),
            jax.ShapeDtypeStruct((2, 2, T, DH), BF),
        ],
        scratch_shapes=[
            pltpu.VMEM((W + n, DH), BF),
            pltpu.VMEM((W + n, DH), BF),
            pltpu.VMEM((n, DH), BF),
            pltpu.VMEM((n, DH), BF),
            pltpu.VMEM((W + n, DH), F32),
            pltpu.VMEM((W + n, DH), F32),
        ],
        compiler_params=params(),
        cost_estimate=cost(12 * n * 768 * DH, 5 << 20, n * W),
        name="attend",
    )(place, *parts, *pieces, prev)


def after(block, *others):
    return lax.optimization_barrier((block,) + others)[0]


def per_device(hidden, weight, keys, values, d_attended):
    z, yl, co, yh, x = (lax.axis_index(a) for a in AXES)
    quad = [(a, b) for a in range(2) for b in range(2)]
    offsets = [0, 1, 2, 3, 4, -1, -2, -3]
    blocks = []
    for d in offsets:
        there = (z - d) % NZ
        blocks.append(((x - there) % NX) * 2 + ((there // NX) ^ yh))
    rows = [(yl ^ dl) * 2 + (co ^ dc) for dc, dl in quad]
    heads = [(yl ^ dl) * 2 + (co ^ dc) for dl, dc in quad]
    lanes = [(yl ^ dl) * 4 + (yh ^ dy) for dy, dl in quad]
    tail = heads + lanes + [yh, 1 - yh, (z % SEQ_Z == 0).astype(jnp.int32)]
    place = jnp.stack(blocks + rows + tail).astype(jnp.int32)
    place_other = jnp.stack(blocks + rows[2:] + rows[:2] + tail).astype(jnp.int32)

    def weight_piece(dc, dy):
        half = lax.dynamic_slice_in_dim(weight, (yh ^ dy) * DH, DH, 0)
        return jnp.concatenate(
            [
                lax.dynamic_slice_in_dim(half, ((yl ^ dl) * 2 + (co ^ dc)) * DH, DH, 1)
                for dl in range(2)
            ],
            axis=1,
        )

    sent = [weight_piece(dc, dy) for dc, dy in quad]
    got = [sent[0], move(sent[1], yh=1), move(sent[2], co=1), move(sent[3], co=1, yh=1)]
    mine = jnp.concatenate(got[:2], axis=1)
    theirs = jnp.concatenate(got[2:], axis=1)
    shard = jnp.concatenate(
        [jnp.where(co == 0, mine, theirs), jnp.where(co == 0, theirs, mine)], axis=0
    )

    def hidden_piece(dy, dl):
        part = lax.dynamic_slice_in_dim(hidden, (yl ^ dl) * 2 * T, 2 * T, 1)
        part = part.reshape(T, 2, 2, DH)
        return lax.dynamic_index_in_dim(part, yh ^ dy, 2, keepdims=False).reshape(T, T)

    mixed = [hidden_piece(dy, dl) for dy, dl in quad]
    mixed = [mixed[0]] + [move(mixed[k], yh=quad[k][0], yl=quad[k][1]) for k in (1, 2, 3)]
    mixed = jnp.stack(mixed).reshape(2, 2, T, T)
    own = [move(mixed, dx=dx) if dx else mixed for dx in range(NX)]

    pieces = []
    for k, (dl, dc) in enumerate(quad):
        piece = jnp.stack(
            [lax.dynamic_slice_in_dim(a, heads[k] * DH, DH, 1) for a in (keys, values, d_attended)]
        )
        pieces.append(move(piece, yl=dl, co=dc) if k else piece)

    up = down = shard
    ups, downs = [], []
    for d in range(1, 5):
        if d == 4:
            up, own[1], own[2], own[3] = lax.optimization_barrier((up, own[1], own[2], own[3]))
        up = move(up, dz=1)
        ups.append(up)
        if d < 4:
            down = move(down, dz=-1)
            downs.append(down)
    weights = [shard] + ups + downs

    own = jnp.stack(own).reshape(8, 2, T, T)
    other = move(own, co=1)
    low = jnp.where(yl == 1, jnp.stack(pieces[:2]), jnp.stack(pieces[2:]))[:, :2]
    prev = move(jnp.where(co == 0, low, low[::-1]), dz=1)
    own = after(own, prev, *pieces)

    parts = query_part(place, own, other, weights)
    parts = [parts[0]] + [move(parts[k], yh=k // 2, yl=k % 2) for k in range(1, 4)]
    attended, dq, dkv, dprev = attend(place, parts, pieces, prev)
    dq = [dq] + [move(dq, yh=k // 2, yl=k % 2) for k in range(1, 4)]

    away = move(d_hidden_part(place_other, dq, weights), co=1)
    sums = d_weight_part(place, own, other, dq)
    near = d_hidden_part(place, dq, weights)
    total = (near.astype(F32) + away.astype(F32)).astype(BF).reshape(NX, 2, 2, T, T)

    def add(a, b):
        return (a.astype(F32) + b.astype(F32)).astype(BF)

    up, down = sums[7], sums[4]
    for d in range(4, 0, -1):
        if d == 3:
            up, down, total = lax.optimization_barrier((up, down, total))
        down = move(down, dz=-1)
        if d > 1:
            down = add(down, sums[d - 1])
        if d < 4:
            up = move(up, dz=1)
            if d > 1:
                up = add(up, sums[4 + d - 1])
    shard = (up.astype(F32) + down.astype(F32) + sums[0].astype(F32)).astype(BF)

    line = total[0].astype(F32)
    for dx in range(1, NX):
        line = line + move(total[dx], dx=-dx).astype(F32)
    line = line.astype(BF)
    shard, line = lax.optimization_barrier((shard, line))
    back = [line[dy, dl] for dy, dl in quad]
    back = [back[0]] + [move(back[k], yh=quad[k][0], yl=quad[k][1]) for k in (1, 2, 3)]
    d_hidden = in_vmem(
        d_hidden_kernel_last, "d_hidden_last", cost(0, 1 << 20), [((T, 8 * DH), BF)], place, *back
    )[0]

    def weight_back(dc, dy):
        block = lax.dynamic_slice_in_dim(shard, (co ^ dc) * DH, DH, 0)
        block = block[:, dy * T : (dy + 1) * T]
        return move(block, co=dc, yh=dy) if dc or dy else block

    back = [weight_back(dc, dy) for dy, dc in quad]
    d_weight = in_vmem(
        d_weight_kernel_last, "d_weight_last", cost(0, 1 << 19), [((T, 4 * DH), BF)], place, *back
    )[0]

    late = move(dprev, dz=-1).astype(F32)
    outs = []
    for k, (dl, dc) in enumerate(quad):
        half = lax.dynamic_index_in_dim(late, co ^ dc, 0, keepdims=False)
        grads = dkv[k] + jnp.where((yl ^ dl) == 1, half, 0.0)
        piece = jnp.concatenate([attended[k][None], grads.astype(BF)], axis=0)
        outs.append(move(piece, yl=dl, co=dc) if k else piece)
    out, d_keys, d_values = in_vmem(
        attended_kernel, "attended_last", cost(0, 1 << 20), [((T, 4 * DH), BF)] * 3, place, *outs
    )
    return out, d_hidden, d_weight, d_keys, d_values


def solution(mesh):
    grid = Mesh(mesh.devices.reshape(SIZES), AXES)
    spec = P(("z", "yl", "co"), ("yh", "x"))
    return jax.shard_map(
        per_device, mesh=grid, in_specs=(spec,) * 5, out_specs=(spec,) * 5, check_vma=False
    )
```

```python
import jax
import jax.numpy as jnp
from jax import lax
from jax.experimental import pallas as pl
from jax.experimental.pallas import tpu as pltpu
from jax.sharding import Mesh, PartitionSpec as P

DH = 128
W = 512
SEQ_Z = 4
AXES = ("z", "yl", "co", "yh", "x")
SIZES = (8, 2, 2, 2, 4)
NZ, NX = 8, 4
T = 256
SCALE = 1.0 / DH**0.5
LOG2E = 1.4426950408889634
BF = jnp.bfloat16
F32 = jnp.float32
VMEM = 56 * 1024 * 1024


def route(target):
    pairs = []
    for i in range(256):
        rest, place = i, []
        for size in SIZES[::-1]:
            place.append(rest % size)
            rest //= size
        there = target(*place[::-1])
        j = 0
        for size, c in zip(SIZES, there):
            j = j * size + c % size
        pairs.append((i, j))
    return pairs


def move(block, dz=0, yl=0, co=0, yh=0, dx=0):
    pairs = route(lambda z, a, b, c, x: (z + dz, a ^ yl, b ^ co, c ^ yh, x + dx))
    return lax.ppermute(block, AXES, pairs)


def params():
    return pltpu.CompilerParams(vmem_limit_bytes=VMEM)


def cost(flops, bytes_accessed, exps=0):
    return pl.CostEstimate(flops=flops, bytes_accessed=bytes_accessed, transcendentals=exps)


def mm(a, b, dims):
    return lax.dot_general(a, b, (dims, ((), ())), preferred_element_type=F32)


OFFSETS = (0, 1, 2, 3, 4, -1, -2, -3)


def fill(scratch, refs):
    for r, d in enumerate(OFFSETS):
        scratch[d % NZ] = refs[r][...]


def feature_block(tokens, i, dl):
    dx, dy = i // 2, i % 2
    if dx == 2:
        return tokens[3 + dy][dl]
    return tokens[(0, 1, 0, 2)[dx]][dy, dl]


def query_kernel(place_ref, *refs):
    own, other, weights, outs, scratch = refs[:5], refs[5:10], refs[10:18], refs[18:22], refs[22]
    fill(scratch, weights)
    w = jnp.concatenate([scratch[place_ref[i]] for i in range(8)], axis=0)
    for dc, tokens in enumerate((own, other)):
        for dl in range(2):
            h = jnp.concatenate([feature_block(tokens, i, dl) for i in range(8)], axis=1)
            part = mm(h, w, ((1,), (0,))).astype(BF)
            row = pl.multiple_of(place_ref[8 + dc * 2 + dl] * T, T)
            for k in range(4):
                outs[k][pl.ds(row, T), :] = part[:, k * DH : (k + 1) * DH]


def in_vmem(kernel, name, work, outs, *args, scratch=()):
    vm = pl.BlockSpec(memory_space=pltpu.VMEM)
    return pl.pallas_call(
        kernel,
        in_specs=[pl.BlockSpec(memory_space=pltpu.SMEM)] + [vm] * (len(args) - 1),
        out_specs=[vm] * len(outs),
        out_shape=[jax.ShapeDtypeStruct(shape, kind) for shape, kind in outs],
        scratch_shapes=scratch,
        compiler_params=params(),
        cost_estimate=work,
        name=name,
    )(*args)


def query_part(place, own, other, weights):
    work = cost(2 * 1024 * 2048 * 512, 7 << 20)
    scratch = [pltpu.VMEM((NZ, T, 4 * DH), BF)]
    outs = [((4 * T, DH), BF)] * 4
    return in_vmem(
        query_kernel, "query_part", work, outs, place, *own, *other, *weights, scratch=scratch
    )


def d_hidden_block(place_ref, refs, scratch, dl, i):
    row = pl.multiple_of(place_ref[8 + dl] * T, T)
    dq = jnp.concatenate([refs[k][pl.ds(row, T), :] for k in range(4)], axis=1)
    return mm(dq, scratch[place_ref[i]], ((1,), (1,)))


def d_hidden_near_kernel(place_ref, *refs):
    away_ref, outs, scratch = refs[12], refs[13:18], refs[18]
    fill(scratch, refs[4:12])
    for dl in range(2):
        for i in range(8):
            part = d_hidden_block(place_ref, refs, scratch, dl, i)
            part = (part + away_ref[i, dl].astype(F32)).astype(BF)
            if i // 2 == 2:
                outs[3 + i % 2][dl] = part
            else:
                outs[(0, 1, 0, 2)[i // 2]][i % 2, dl] = part


def d_hidden_near(place, dq, weights, away):
    work = cost(1024 * 2048 * 512, 5 << 20)
    scratch = [pltpu.VMEM((NZ, T, 4 * DH), BF)]
    outs = [((2, 2, T, T), BF)] * 3 + [((2, T, T), BF)] * 2
    return in_vmem(
        d_hidden_near_kernel, "d_hidden_near", work, outs, place, *dq, *weights, away,
        scratch=scratch,
    )


def all_dq(place_ref, refs):
    return jnp.concatenate(
        [
            jnp.concatenate(
                [
                    ref[pl.ds(pl.multiple_of(place_ref[8 + j] * T, T), T), :]
                    for ref in refs
                ],
                axis=1,
            )
            for j in range(4)
        ],
        axis=0,
    )


def all_tokens(own, other, i):
    return jnp.concatenate(
        [feature_block(tokens, i, dl) for tokens in (own, other) for dl in range(2)], axis=0
    )


def d_hidden_away_kernel(place_ref, *refs):
    own, other, outs, scratch = refs[12:17], refs[17:22], refs[22:24], refs[24]
    fill(scratch, refs[4:12])
    for i in range(8):

        @pl.when(place_ref[i] == 4)
        def _(i=i):
            dq = all_dq(place_ref, refs[:4])
            outs[1][...] = mm(all_tokens(other, own, i), dq, ((0,), (0,))).astype(BF)

    for dl in range(2):
        for i in range(8):
            outs[0][i, dl] = d_hidden_block(place_ref, refs, scratch, dl, i).astype(BF)


def d_hidden_away(place, own, other, dq, weights):
    work = cost(1024 * 2048 * 512, 5 << 20)
    scratch = [pltpu.VMEM((NZ, T, 4 * DH), BF)]
    outs = [((8, 2, T, T), BF), ((T, 4 * DH), BF)]
    return in_vmem(
        d_hidden_away_kernel, "d_hidden_away", work, outs, place, *dq, *weights, *own, *other,
        scratch=scratch,
    )


def d_weight_kernel(place_ref, *refs):
    own, other, outs, scratch = refs[:5], refs[5:10], refs[14:21], refs[21]
    dq = all_dq(place_ref, refs[10:14])
    for i in range(8):
        scratch[place_ref[i]] = mm(all_tokens(own, other, i), dq, ((0,), (0,))).astype(BF)
    for out, d in zip(outs, (0, 1, 2, 3, -1, -2, -3)):
        out[...] = scratch[d % NZ]


def d_weight_part(place, own, other, dq):
    work = cost(2 * 1024 * 2048 * 512, 7 << 20)
    scratch = [pltpu.VMEM((NZ, T, 4 * DH), BF)]
    outs = [((T, 4 * DH), BF)] * 7
    return in_vmem(
        d_weight_kernel, "d_weight_part", work, outs, place, *own, *other, *dq, scratch=scratch
    )


def attended_kernel(place_ref, own_ref, core_ref, y_ref, *outs):
    for k, ref in enumerate((own_ref, core_ref.at[0], y_ref.at[0], core_ref.at[1])):
        at = pl.multiple_of(place_ref[12 + k] * DH, DH)
        for j in range(3):
            outs[j][:, pl.ds(at, DH)] = ref[j]


def d_hidden_kernel_last(place_ref, *refs):
    for k in range(4):
        at = place_ref[16 + k]
        for co in range(2):
            first = pl.multiple_of((at + co * 2) * DH, DH)
            refs[4][:, pl.ds(first, DH)] = refs[k][:, co * DH : (co + 1) * DH]


def d_weight_kernel_last(place_ref, *refs):
    for dy in range(2):
        row = pl.multiple_of(place_ref[20 + dy] * DH, DH)
        for dc in range(2):
            for dl in range(2):
                at = pl.multiple_of(place_ref[12 + dl * 2 + dc] * DH, DH)
                refs[4][pl.ds(row, DH), pl.ds(at, DH)] = refs[dy * 2 + dc][
                    :, dl * DH : (dl + 1) * DH
                ]


def attend_kernel(
    place_ref, q0_ref, q1_ref, q2_ref, q3_ref, p0_ref, p1_ref, p2_ref, prev_ref,
    out_ref, dq_ref, dkv_ref, dprev_ref, k_ref, v_ref, g_ref, o_ref, dk_ref, dv_ref,
):
    tokens = [pl.multiple_of(place_ref[12 + k] * T, T) for k in range(4)]
    for half in range(2):
        k_ref[half * T : (half + 1) * T] = prev_ref[half, 0]
        v_ref[half * T : (half + 1) * T] = prev_ref[half, 1]
    for row, ref in zip(tokens, (p0_ref, p1_ref.at[0], p2_ref.at[0], p2_ref.at[1])):
        k_ref[pl.ds(W + row, T), :] = ref[0]
        v_ref[pl.ds(W + row, T), :] = ref[1]
        g_ref[pl.ds(row, T), :] = ref[2]
    dk_ref[...] = jnp.zeros_like(dk_ref)
    dv_ref[...] = jnp.zeros_like(dv_ref)
    inside = place_ref[22] == 0
    rows = lax.broadcasted_iota(jnp.int32, (T, T), 0)
    cols = lax.broadcasted_iota(jnp.int32, (T, T), 1)
    old = cols > rows
    for i in range(4):
        at = slice(i * T, (i + 1) * T)
        window = slice(i * T, i * T + W + T)
        q = (
            q0_ref[at].astype(F32) + q1_ref[at].astype(F32)
            + q2_ref[at].astype(F32) + q3_ref[at].astype(F32)
        ).astype(BF)
        g = g_ref[at]
        k = k_ref[window]
        v = v_ref[window]
        s = mm(q, k, ((1,), (1,)))
        sa, sb, sc = s[:, :T], s[:, T : 2 * T], s[:, 2 * T :]
        if i < 2:
            sa = jnp.where(inside, sa, -1e30)
        if i < 1:
            sb = jnp.where(inside, sb, -1e30)
        sm = jnp.where(old, sa, sc)
        top = jnp.max(jnp.maximum(sm, sb), axis=1, keepdims=True)
        em = jnp.exp2((sm - top) * (SCALE * LOG2E))
        eb = jnp.exp2((sb - top) * (SCALE * LOG2E))
        inv = 1.0 / jnp.sum(em + eb, axis=1, keepdims=True)
        pm = em * inv
        pb = eb * inv
        prob = jnp.concatenate(
            [
                jnp.where(old, pm, 0.0).astype(BF),
                pb.astype(BF),
                jnp.where(old, 0.0, pm).astype(BF),
            ],
            axis=1,
        )
        o_ref[at] = mm(prob, v, ((1,), (0,))).astype(BF)
        dp = mm(g, v, ((1,), (1,)))
        dpm = jnp.where(old, dp[:, :T], dp[:, 2 * T :])
        dpb = dp[:, T : 2 * T]
        delta = jnp.sum(pm * dpm + pb * dpb, axis=1, keepdims=True)
        dsm = pm * (dpm - delta) * SCALE
        dsb = pb * (dpb - delta) * SCALE
        ds = jnp.concatenate(
            [
                jnp.where(old, dsm, 0.0).astype(BF),
                dsb.astype(BF),
                jnp.where(old, 0.0, dsm).astype(BF),
            ],
            axis=1,
        )
        dq_ref[at] = mm(ds, k, ((1,), (0,))).astype(BF)
        dk_ref[window] += mm(ds, q, ((0,), (0,)))
        dv_ref[window] += mm(prob, g, ((0,), (0,)))
    for half in range(2):
        dprev_ref[half, 0] = dk_ref[half * T : (half + 1) * T].astype(BF)
        dprev_ref[half, 1] = dv_ref[half * T : (half + 1) * T].astype(BF)
    for k, row in enumerate(tokens):
        out_ref[k] = o_ref[pl.ds(row, T), :]
        dkv_ref[k, 0] = dk_ref[pl.ds(W + row, T), :]
        dkv_ref[k, 1] = dv_ref[pl.ds(W + row, T), :]


def attend(place, parts, pieces, prev):
    vm = pl.BlockSpec(memory_space=pltpu.VMEM)
    n = 4 * T
    return pl.pallas_call(
        attend_kernel,
        in_specs=[pl.BlockSpec(memory_space=pltpu.SMEM)] + [vm] * 8,
        out_specs=[vm] * 4,
        out_shape=[
            jax.ShapeDtypeStruct((4, T, DH), BF),
            jax.ShapeDtypeStruct((n, DH), BF),
            jax.ShapeDtypeStruct((4, 2, T, DH), F32),
            jax.ShapeDtypeStruct((2, 2, T, DH), BF),
        ],
        scratch_shapes=[
            pltpu.VMEM((W + n, DH), BF),
            pltpu.VMEM((W + n, DH), BF),
            pltpu.VMEM((n, DH), BF),
            pltpu.VMEM((n, DH), BF),
            pltpu.VMEM((W + n, DH), F32),
            pltpu.VMEM((W + n, DH), F32),
        ],
        compiler_params=params(),
        cost_estimate=cost(12 * n * 768 * DH, 5 << 20, n * W),
        name="attend",
    )(place, *parts, *pieces, prev)


def tie(*groups):
    flat = iter(lax.optimization_barrier([a for group in groups for a in group]))
    return [[next(flat) for _ in group] for group in groups]


def per_device(hidden, weight, keys, values, d_attended):
    z, yl, co, yh, x = (lax.axis_index(a) for a in AXES)
    quad = [(a, b) for a in range(2) for b in range(2)]
    blocks = [
        (z - ((yh ^ dy) * NX + (x - dx) % NX)) % NZ for dx in range(NX) for dy in range(2)
    ]
    rows = [(yl ^ dl) * 2 + (co ^ dc) for dc, dl in quad]
    heads = [(yl ^ dl) * 2 + (co ^ dc) for dl, dc in quad]
    lanes = [(yl ^ dl) * 4 + (yh ^ dy) for dy, dl in quad]
    tail = heads + lanes + [yh, 1 - yh, (z % SEQ_Z == 0).astype(jnp.int32)]
    place = jnp.stack(blocks + rows + tail).astype(jnp.int32)
    place_other = jnp.stack(blocks + rows[2:] + rows[:2] + tail).astype(jnp.int32)

    def weight_piece(dc, dy):
        half = lax.dynamic_slice_in_dim(weight, (yh ^ dy) * DH, DH, 0)
        return jnp.concatenate(
            [
                lax.dynamic_slice_in_dim(half, ((yl ^ dl) * 2 + (co ^ dc)) * DH, DH, 1)
                for dl in range(2)
            ],
            axis=1,
        )

    kvd = [
        jnp.stack(
            [lax.dynamic_slice_in_dim(a, heads[k] * DH, DH, 1) for a in (keys, values, d_attended)]
        )
        for k in range(4)
    ]

    sent = [weight_piece(dc, dy) for dc, dy in quad]
    got = [sent[0], move(sent[1], yh=1), move(sent[2], co=1), move(sent[3], co=1, yh=1)]
    swapped = move(jnp.stack([kvd[1], kvd[3]]), co=1)
    mine = jnp.concatenate(got[:2], axis=1)
    theirs = jnp.concatenate(got[2:], axis=1)
    shard = jnp.concatenate(
        [jnp.where(co == 0, mine, theirs), jnp.where(co == 0, theirs, mine)], axis=0
    )

    def hidden_piece(dy, dl):
        part = lax.dynamic_slice_in_dim(hidden, (yl ^ dl) * 2 * T, 2 * T, 1)
        part = part.reshape(T, 2, 2, DH)
        return lax.dynamic_index_in_dim(part, yh ^ dy, 2, keepdims=False).reshape(T, T)

    def step_up(a):
        return move(a, dz=1)

    def step_down(a):
        return move(a, dz=-1)

    ups, downs = [step_up(shard)], [step_down(shard)]
    mixed = [hidden_piece(dy, dl) for dy, dl in quad]
    mixed = [mixed[0]] + [move(mixed[k], yh=quad[k][0], yl=quad[k][1]) for k in (1, 2, 3)]
    mixed = jnp.stack(mixed).reshape(2, 2, T, T)

    (up,), (down,), (mixed,), (swapped,) = tie(ups, downs, (mixed,), (swapped,))

    ups.append(step_up(up))
    downs.append(step_down(down))
    far = move(shard, dz=4)
    own = [mixed, move(mixed, dx=1), move(mixed, dx=-1)]
    (up, down, far), own = tie((ups[1], downs[1], far), own)

    ups.append(step_up(up))
    downs.append(step_down(down))
    own += [move(own[1][0], dx=1), move(own[2][1], dx=-1)]
    pieces = [kvd[0], swapped, move(jnp.stack([kvd[2], swapped[1]]), yl=1)]
    (up, down), own, pieces = tie((ups[2], downs[2]), own, pieces)
    ups[2], downs[2] = up, down

    other = [move(block, co=1) for block in own]
    weights = [shard] + ups + [far] + downs
    own, other, weights, pieces = tie(own, other, weights, pieces)
    low = jnp.where(yl == 1, jnp.stack([pieces[0][:2], pieces[1][0, :2]]), pieces[2][:, :2])
    prev = move(jnp.where(co == 0, low, low[::-1]), dz=1)

    parts = query_part(place, own, other, weights)
    parts = [parts[0]] + [move(parts[k], yh=k // 2, yl=k % 2) for k in range(1, 4)]
    attended, dq, dkv, dprev = attend(place, parts, pieces, prev)
    dq = [dq] + [move(dq, yh=k // 2, yl=k % 2) for k in range(1, 4)]

    away, far = d_hidden_away(place_other, own, other, dq, weights)
    away, far = move(away, co=1), move(far, dz=4)
    sums = d_weight_part(place, own, other, dq)
    near = d_hidden_near(place, dq, weights, away)

    def add(a, b):
        return (a.astype(F32) + b.astype(F32)).astype(BF)

    up, down = step_up(sums[6]), step_down(sums[3])
    late = move(dprev, dz=-1)
    (up, down, late), near, sums = tie((up, down, late), near, sums)
    up, down = add(up, sums[5]), add(down, sums[2])

    outs = []
    for k, (dl, dc) in enumerate(quad):
        half = lax.dynamic_index_in_dim(late, co ^ dc, 0, keepdims=False).astype(F32)
        grads = dkv[k] + jnp.where((yl ^ dl) == 1, half, 0.0)
        outs.append(jnp.concatenate([attended[k][None], grads.astype(BF)], axis=0))

    up, down = step_up(up), step_down(down)
    right = move(near[3], dx=1)
    left = move(near[4], dx=-1)
    crossed = move(jnp.stack(outs[2:]), yl=1)
    (up, down, right, left, crossed), outs, sums = tie((up, down, right, left, crossed), outs, sums)
    right = jnp.stack([add(near[2][0], right), near[2][1]])
    left = jnp.stack([near[1][0], add(near[1][1], left)])
    up, down = add(up, sums[4]), add(down, sums[1])

    up, down = step_up(up), step_down(down)
    line = [near[0], move(right, dx=1), move(left, dx=-1)]
    outs = [outs[0], move(jnp.stack([outs[1], crossed[1]]), co=1), crossed]
    (up, down, far), line, outs, sums = tie((up, down, far), line, outs, sums)

    result = in_vmem(
        attended_kernel, "attended_last", cost(0, 1 << 20), [((T, 4 * DH), BF)] * 3, place, *outs
    )
    line = sum(block.astype(F32) for block in line).astype(BF)
    back = [line[dy, dl] for dy, dl in quad]
    back = [back[0]] + [move(back[k], yh=quad[k][0], yl=quad[k][1]) for k in (1, 2, 3)]
    d_hidden = in_vmem(
        d_hidden_kernel_last, "d_hidden_last", cost(0, 1 << 20), [((T, 8 * DH), BF)], place, *back
    )[0]

    shard = sum(block.astype(F32) for block in (up, down, far, sums[0])).astype(BF)

    def weight_back(dc, dy):
        block = lax.dynamic_slice_in_dim(shard, (co ^ dc) * DH, DH, 0)
        block = block[:, dy * T : (dy + 1) * T]
        return move(block, co=dc, yh=dy) if dc or dy else block

    back = [weight_back(dc, dy) for dy, dc in quad]
    d_weight = in_vmem(
        d_weight_kernel_last, "d_weight_last", cost(0, 1 << 19), [((T, 4 * DH), BF)], place, *back
    )[0]

    return result[0], d_hidden, d_weight, result[1], result[2]


def solution(mesh):
    grid = Mesh(mesh.devices.reshape(SIZES), AXES)
    spec = P(("z", "yl", "co"), ("yh", "x"))
    return jax.shard_map(
        per_device, mesh=grid, in_specs=(spec,) * 5, out_specs=(spec,) * 5, check_vma=False
    )
```

```python
import jax
import jax.numpy as jnp
from jax import lax
from jax.experimental import pallas as pl
from jax.experimental.pallas import tpu as pltpu
from jax.sharding import Mesh, PartitionSpec as P

DH = 128
W = 512
SEQ_Z = 4
AXES = ("z", "yl", "co", "yh", "x")
SIZES = (8, 2, 2, 2, 4)
NZ, NX = 8, 4
T = 256
SCALE = 1.0 / DH**0.5
LOG2E = 1.4426950408889634
BF = jnp.bfloat16
F32 = jnp.float32
VMEM = 56 * 1024 * 1024


def route(target):
    pairs = []
    for i in range(256):
        rest, place = i, []
        for size in SIZES[::-1]:
            place.append(rest % size)
            rest //= size
        there = target(*place[::-1])
        j = 0
        for size, c in zip(SIZES, there):
            j = j * size + c % size
        pairs.append((i, j))
    return pairs


def move(block, dz=0, yl=0, co=0, yh=0, dx=0):
    pairs = route(lambda z, a, b, c, x: (z + dz, a ^ yl, b ^ co, c ^ yh, x + dx))
    return lax.ppermute(block, AXES, pairs)


def params():
    return pltpu.CompilerParams(vmem_limit_bytes=VMEM)


def cost(flops, bytes_accessed, exps=0):
    return pl.CostEstimate(flops=flops, bytes_accessed=bytes_accessed, transcendentals=exps)


def mm(a, b, dims):
    return lax.dot_general(a, b, (dims, ((), ())), preferred_element_type=F32)


def feature_block(tokens, i, dl):
    return tokens[i // 2][i % 2, dl]


def query_kernel(place_ref, *refs):
    own, other, w_ref, outs = refs[:4], refs[4:8], refs[8], refs[9:13]
    w = jnp.concatenate([w_ref[place_ref[i]] for i in range(8)], axis=0)
    for dc, tokens in enumerate((own, other)):
        for dl in range(2):
            h = jnp.concatenate([feature_block(tokens, i, dl) for i in range(8)], axis=1)
            part = mm(h, w, ((1,), (0,))).astype(BF)
            row = pl.multiple_of(place_ref[8 + dc * 2 + dl] * T, T)
            for k in range(4):
                outs[k][pl.ds(row, T), :] = part[:, k * DH : (k + 1) * DH]


def in_vmem(kernel, name, work, outs, *args):
    vm = pl.BlockSpec(memory_space=pltpu.VMEM)
    return pl.pallas_call(
        kernel,
        in_specs=[pl.BlockSpec(memory_space=pltpu.SMEM)] + [vm] * (len(args) - 1),
        out_specs=[vm] * len(outs),
        out_shape=[jax.ShapeDtypeStruct(shape, kind) for shape, kind in outs],
        compiler_params=params(),
        cost_estimate=work,
        name=name,
    )(*args)


def query_part(place, own, other, weights):
    work = cost(2 * 1024 * 2048 * 512, 7 << 20)
    outs = [((4 * T, DH), BF)] * 4
    return in_vmem(query_kernel, "query_part", work, outs, place, *own, *other, weights)


def d_hidden_block(place_ref, refs, dl, i):
    row = pl.multiple_of(place_ref[8 + dl] * T, T)
    dq = jnp.concatenate([refs[k][pl.ds(row, T), :] for k in range(4)], axis=1)
    return mm(dq, refs[4][place_ref[i]], ((1,), (1,)))


def d_hidden_away_kernel(place_ref, *refs):
    for dl in range(2):
        for i in range(8):
            refs[5][i, dl] = d_hidden_block(place_ref, refs, dl, i).astype(BF)


def d_hidden_near_kernel(place_ref, *refs):
    for dl in range(2):
        for i in range(8):
            part = d_hidden_block(place_ref, refs, dl, i)
            refs[6 + i // 2][i % 2, dl] = (part + refs[5][i, dl].astype(F32)).astype(BF)


def d_hidden_away(place, dq, weights):
    work = cost(1024 * 2048 * 512, 5 << 20)
    outs = [((8, 2, T, T), BF)]
    return in_vmem(d_hidden_away_kernel, "d_hidden_away", work, outs, place, *dq, weights)[0]


def d_hidden_near(place, dq, weights, away):
    work = cost(1024 * 2048 * 512, 7 << 20)
    outs = [((2, 2, T, T), BF)] * 4
    return in_vmem(d_hidden_near_kernel, "d_hidden_near", work, outs, place, *dq, weights, away)


def d_weight_kernel(place_ref, *refs):
    own, other, dqs, out_ref = refs[:4], refs[4:8], refs[8:12], refs[12]
    dq = jnp.concatenate(
        [
            jnp.concatenate(
                [
                    ref[pl.ds(pl.multiple_of(place_ref[8 + j] * T, T), T), :]
                    for ref in dqs
                ],
                axis=1,
            )
            for j in range(4)
        ],
        axis=0,
    )
    for i in range(8):
        h = jnp.concatenate(
            [feature_block(tokens, i, dl) for tokens in (own, other) for dl in range(2)], axis=0
        )
        out_ref[place_ref[i]] = mm(h, dq, ((0,), (0,))).astype(BF)


def d_weight_part(place, own, other, dq):
    work = cost(2 * 1024 * 2048 * 512, 7 << 20)
    outs = [((NZ, T, 4 * DH), BF)]
    return in_vmem(d_weight_kernel, "d_weight_part", work, outs, place, *own, *other, *dq)[0]


def attended_kernel(place_ref, own_ref, core_ref, y_ref, *outs):
    for k, ref in enumerate((own_ref, core_ref.at[0], y_ref.at[0], core_ref.at[1])):
        at = pl.multiple_of(place_ref[12 + k] * DH, DH)
        for j in range(3):
            outs[j][:, pl.ds(at, DH)] = ref[j]


def last_kernel(place_ref, *refs):
    for k in range(4):
        at = place_ref[16 + k]
        for co in range(2):
            first = pl.multiple_of((at + co * 2) * DH, DH)
            refs[8][:, pl.ds(first, DH)] = refs[k][:, co * DH : (co + 1) * DH]
    for dy in range(2):
        row = pl.multiple_of(place_ref[20 + dy] * DH, DH)
        for dc in range(2):
            for dl in range(2):
                at = pl.multiple_of(place_ref[12 + dl * 2 + dc] * DH, DH)
                refs[9][pl.ds(row, DH), pl.ds(at, DH)] = refs[4 + dy * 2 + dc][
                    :, dl * DH : (dl + 1) * DH
                ]


def attend_kernel(
    place_ref, q0_ref, q1_ref, q2_ref, q3_ref, p0_ref, p1_ref, p2_ref, prev_ref,
    out_ref, dq_ref, dkv_ref, dprev_ref, k_ref, v_ref, g_ref, o_ref, dk_ref, dv_ref,
):
    tokens = [pl.multiple_of(place_ref[12 + k] * T, T) for k in range(4)]
    for half in range(2):
        k_ref[half * T : (half + 1) * T] = prev_ref[half, 0]
        v_ref[half * T : (half + 1) * T] = prev_ref[half, 1]
    for row, ref in zip(tokens, (p0_ref, p1_ref.at[0], p2_ref.at[0], p2_ref.at[1])):
        k_ref[pl.ds(W + row, T), :] = ref[0]
        v_ref[pl.ds(W + row, T), :] = ref[1]
        g_ref[pl.ds(row, T), :] = ref[2]
    dk_ref[...] = jnp.zeros_like(dk_ref)
    dv_ref[...] = jnp.zeros_like(dv_ref)
    inside = place_ref[22] == 0
    rows = lax.broadcasted_iota(jnp.int32, (T, T), 0)
    cols = lax.broadcasted_iota(jnp.int32, (T, T), 1)
    old = cols > rows
    for i in range(4):
        at = slice(i * T, (i + 1) * T)
        window = slice(i * T, i * T + W + T)
        q = (
            q0_ref[at].astype(F32) + q1_ref[at].astype(F32)
            + q2_ref[at].astype(F32) + q3_ref[at].astype(F32)
        ).astype(BF)
        g = g_ref[at]
        k = k_ref[window]
        v = v_ref[window]
        s = mm(q, k, ((1,), (1,)))
        sa, sb, sc = s[:, :T], s[:, T : 2 * T], s[:, 2 * T :]
        if i < 2:
            sa = jnp.where(inside, sa, -1e30)
        if i < 1:
            sb = jnp.where(inside, sb, -1e30)
        sm = jnp.where(old, sa, sc)
        top = jnp.max(jnp.maximum(sm, sb), axis=1, keepdims=True)
        em = jnp.exp2((sm - top) * (SCALE * LOG2E))
        eb = jnp.exp2((sb - top) * (SCALE * LOG2E))
        inv = 1.0 / jnp.sum(em + eb, axis=1, keepdims=True)
        pm = em * inv
        pb = eb * inv
        prob = jnp.concatenate(
            [
                jnp.where(old, pm, 0.0).astype(BF),
                pb.astype(BF),
                jnp.where(old, 0.0, pm).astype(BF),
            ],
            axis=1,
        )
        o_ref[at] = mm(prob, v, ((1,), (0,))).astype(BF)
        dp = mm(g, v, ((1,), (1,)))
        dpm = jnp.where(old, dp[:, :T], dp[:, 2 * T :])
        dpb = dp[:, T : 2 * T]
        delta = jnp.sum(pm * dpm + pb * dpb, axis=1, keepdims=True)
        dsm = pm * (dpm - delta) * SCALE
        dsb = pb * (dpb - delta) * SCALE
        ds = jnp.concatenate(
            [
                jnp.where(old, dsm, 0.0).astype(BF),
                dsb.astype(BF),
                jnp.where(old, 0.0, dsm).astype(BF),
            ],
            axis=1,
        )
        dq_ref[at] = mm(ds, k, ((1,), (0,))).astype(BF)
        dk_ref[window] += mm(ds, q, ((0,), (0,)))
        dv_ref[window] += mm(prob, g, ((0,), (0,)))
    for half in range(2):
        dprev_ref[half, 0] = dk_ref[half * T : (half + 1) * T].astype(BF)
        dprev_ref[half, 1] = dv_ref[half * T : (half + 1) * T].astype(BF)
    for k, row in enumerate(tokens):
        out_ref[k] = o_ref[pl.ds(row, T), :]
        dkv_ref[k, 0] = dk_ref[pl.ds(W + row, T), :]
        dkv_ref[k, 1] = dv_ref[pl.ds(W + row, T), :]


def attend(place, parts, pieces, prev):
    vm = pl.BlockSpec(memory_space=pltpu.VMEM)
    n = 4 * T
    return pl.pallas_call(
        attend_kernel,
        in_specs=[pl.BlockSpec(memory_space=pltpu.SMEM)] + [vm] * 8,
        out_specs=[vm] * 4,
        out_shape=[
            jax.ShapeDtypeStruct((4, T, DH), BF),
            jax.ShapeDtypeStruct((n, DH), BF),
            jax.ShapeDtypeStruct((4, 2, T, DH), F32),
            jax.ShapeDtypeStruct((2, 2, T, DH), BF),
        ],
        scratch_shapes=[
            pltpu.VMEM((W + n, DH), BF),
            pltpu.VMEM((W + n, DH), BF),
            pltpu.VMEM((n, DH), BF),
            pltpu.VMEM((n, DH), BF),
            pltpu.VMEM((W + n, DH), F32),
            pltpu.VMEM((W + n, DH), F32),
        ],
        compiler_params=params(),
        cost_estimate=cost(12 * n * 768 * DH, 5 << 20, n * W),
        name="attend",
    )(place, *parts, *pieces, prev)


def tie(*groups):
    flat = iter(lax.optimization_barrier([a for group in groups for a in group]))
    return [[next(flat) for _ in group] for group in groups]


def per_device(hidden, weight, keys, values, d_attended):
    z, yl, co, yh, x = (lax.axis_index(a) for a in AXES)
    quad = [(a, b) for a in range(2) for b in range(2)]
    blocks = [(yh ^ dy) * NX + (x - dx) % NX for dx in range(NX) for dy in range(2)]
    rows = [(yl ^ dl) * 2 + (co ^ dc) for dc, dl in quad]
    heads = [(yl ^ dl) * 2 + (co ^ dc) for dl, dc in quad]
    lanes = [(yl ^ dl) * 4 + (yh ^ dy) for dy, dl in quad]
    tail = heads + lanes + [yh, 1 - yh, (z % SEQ_Z == 0).astype(jnp.int32)]
    place = jnp.stack(blocks + rows + tail).astype(jnp.int32)
    place_other = jnp.stack(blocks + rows[2:] + rows[:2] + tail).astype(jnp.int32)

    def weight_piece(dc, dy):
        half = lax.dynamic_slice_in_dim(weight, (yh ^ dy) * DH, DH, 0)
        return jnp.concatenate(
            [
                lax.dynamic_slice_in_dim(half, ((yl ^ dl) * 2 + (co ^ dc)) * DH, DH, 1)
                for dl in range(2)
            ],
            axis=1,
        )

    kvd = [
        jnp.stack(
            [lax.dynamic_slice_in_dim(a, heads[k] * DH, DH, 1) for a in (keys, values, d_attended)]
        )
        for k in range(4)
    ]

    sent = [weight_piece(dc, dy) for dc, dy in quad]
    got = [sent[0], move(sent[1], yh=1), move(sent[2], co=1), move(sent[3], co=1, yh=1)]
    mine = jnp.concatenate(got[:2], axis=1)
    theirs = jnp.concatenate(got[2:], axis=1)
    shard = jnp.concatenate(
        [jnp.where(co == 0, mine, theirs), jnp.where(co == 0, theirs, mine)], axis=0
    )

    def hidden_piece(dy, dl):
        part = lax.dynamic_slice_in_dim(hidden, (yl ^ dl) * 2 * T, 2 * T, 1)
        part = part.reshape(T, 2, 2, DH)
        return lax.dynamic_index_in_dim(part, yh ^ dy, 2, keepdims=False).reshape(T, T)

    mixed = [hidden_piece(dy, dl) for dy, dl in quad]
    mixed = [mixed[0]] + [move(mixed[k], yh=quad[k][0], yl=quad[k][1]) for k in (1, 2, 3)]
    mixed = jnp.stack(mixed).reshape(2, 2, T, T)

    own = [move(mixed, dx=dx) if dx else mixed for dx in range(NX)]
    own, kvd = tie(own, kvd)
    other = [move(block, co=1) for block in own]
    swapped = move(jnp.stack([kvd[1], kvd[3]]), co=1)
    pieces = [kvd[0], swapped, move(jnp.stack([kvd[2], swapped[1]]), yl=1)]
    weights = lax.all_gather(shard, "z", axis=0, tiled=False)
    own, other, (weights,) = tie(own, other, (weights,))

    parts = query_part(place, own, other, weights)
    parts, pieces = tie(parts, pieces)
    low = jnp.where(yl == 1, jnp.stack([pieces[0][:2], pieces[1][0, :2]]), pieces[2][:, :2])
    prev = move(jnp.where(co == 0, low, low[::-1]), dz=1)

    parts = [parts[0]] + [move(parts[k], yh=k // 2, yl=k % 2) for k in range(1, 4)]
    attended, dq, dkv, dprev = attend(place, parts, pieces, prev)
    dq = [dq] + [move(dq, yh=k // 2, yl=k % 2) for k in range(1, 4)]

    late = move(dprev, dz=-1)
    dq, (late,) = tie(dq, (late,))
    sums = d_weight_part(place, own, other, dq)
    shard = lax.psum_scatter(sums.reshape(NZ * T, 4 * DH), "z", scatter_dimension=0, tiled=True)
    away = move(d_hidden_away(place_other, dq, weights), co=1)
    near = d_hidden_near(place, dq, weights, away)

    outs = []
    for k, (dl, dc) in enumerate(quad):
        half = lax.dynamic_index_in_dim(late, co ^ dc, 0, keepdims=False).astype(F32)
        grads = dkv[k] + jnp.where((yl ^ dl) == 1, half, 0.0)
        outs.append(jnp.concatenate([attended[k][None], grads.astype(BF)], axis=0))

    crossed = move(jnp.stack(outs[2:]), yl=1)
    outs = [outs[0], move(jnp.stack([outs[1], crossed[1]]), co=1), crossed]
    result = in_vmem(
        attended_kernel, "attended_last", cost(0, 1 << 20), [((T, 4 * DH), BF)] * 3, place, *outs
    )

    line = [near[0]] + [move(near[dx], dx=-dx) for dx in range(1, NX)]
    line, result = tie(line, result)
    line = sum(block.astype(F32) for block in line).astype(BF)
    back = [line[dy, dl] for dy, dl in quad]
    back = [back[0]] + [move(back[k], yh=quad[k][0], yl=quad[k][1]) for k in (1, 2, 3)]
    def weight_back(dc, dy):
        block = lax.dynamic_slice_in_dim(shard, (co ^ dc) * DH, DH, 0)
        block = block[:, dy * T : (dy + 1) * T]
        return move(block, co=dc, yh=dy) if dc or dy else block

    back += [weight_back(dc, dy) for dy, dc in quad]
    d_hidden, d_weight = in_vmem(
        last_kernel, "last", cost(0, 1 << 20), [((T, 8 * DH), BF), ((T, 4 * DH), BF)], place, *back
    )

    return result[0], d_hidden, d_weight, result[1], result[2]


def solution(mesh):
    grid = Mesh(mesh.devices.reshape(SIZES), AXES)
    spec = P(("z", "yl", "co"), ("yh", "x"))
    return jax.shard_map(
        per_device, mesh=grid, in_specs=(spec,) * 5, out_specs=(spec,) * 5, check_vma=False
    )
```

```python
import jax
import jax.numpy as jnp
from jax import lax
from jax.experimental import pallas as pl
from jax.experimental.pallas import tpu as pltpu
from jax.sharding import Mesh, PartitionSpec as P

DH = 128
W = 512
SEQ_Z = 4
AXES = ("z", "yl", "co", "yh", "x")
SIZES = (8, 2, 2, 2, 4)
NZ, NX = 8, 4
T = 256
SCALE = 1.0 / DH**0.5
LOG2E = 1.4426950408889634
BF = jnp.bfloat16
F32 = jnp.float32


def route(target):
    pairs = []
    for i in range(256):
        rest, place = i, []
        for size in SIZES[::-1]:
            place.append(rest % size)
            rest //= size
        there = target(*place[::-1])
        j = 0
        for size, c in zip(SIZES, there):
            j = j * size + c % size
        pairs.append((i, j))
    return pairs


def move(block, dz=0, yl=0, co=0, yh=0, dx=0):
    pairs = route(lambda z, a, b, c, x: (z + dz, a ^ yl, b ^ co, c ^ yh, x + dx))
    return lax.ppermute(block, AXES, pairs)


def params(mebibytes=20):
    return pltpu.CompilerParams(vmem_limit_bytes=mebibytes * 1024 * 1024)


def cost(flops, bytes_accessed, exps=0):
    return pl.CostEstimate(flops=flops, bytes_accessed=bytes_accessed, transcendentals=exps)


def mm(a, b, dims):
    return lax.dot_general(a, b, (dims, ((), ())), preferred_element_type=F32)


def feature_block(tokens, i, dl):
    return tokens[i // 2][i % 2, dl]


def query_kernel(place_ref, *refs):
    own, other, w_ref, outs = refs[:4], refs[4:8], refs[8], refs[9:13]
    w = jnp.concatenate([w_ref[place_ref[i]] for i in range(8)], axis=0)
    for dc, tokens in enumerate((own, other)):
        for dl in range(2):
            h = jnp.concatenate([feature_block(tokens, i, dl) for i in range(8)], axis=1)
            part = mm(h, w, ((1,), (0,))).astype(BF)
            row = pl.multiple_of(place_ref[8 + dc * 2 + dl] * T, T)
            for k in range(4):
                outs[k][pl.ds(row, T), :] = part[:, k * DH : (k + 1) * DH]


def in_vmem(kernel, name, work, outs, *args, room=20):
    vm = pl.BlockSpec(memory_space=pltpu.VMEM)
    return pl.pallas_call(
        kernel,
        in_specs=[pl.BlockSpec(memory_space=pltpu.SMEM)] + [vm] * (len(args) - 1),
        out_specs=[vm] * len(outs),
        out_shape=[jax.ShapeDtypeStruct(shape, kind) for shape, kind in outs],
        compiler_params=params(room),
        cost_estimate=work,
        name=name,
    )(*args)


def query_part(place, own, other, weights):
    work = cost(2 * 1024 * 2048 * 512, 7 << 20)
    outs = [((4 * T, DH), BF)] * 4
    return in_vmem(query_kernel, "query_part", work, outs, place, *own, *other, weights, room=56)


def d_hidden_block(place_ref, refs, dl, i):
    row = pl.multiple_of(place_ref[8 + dl] * T, T)
    dq = jnp.concatenate([refs[k][pl.ds(row, T), :] for k in range(4)], axis=1)
    return mm(dq, refs[4][place_ref[i]], ((1,), (1,)))


def d_hidden_away_kernel(place_ref, *refs):
    for dl in range(2):
        for i in range(8):
            refs[5][i, dl] = d_hidden_block(place_ref, refs, dl, i).astype(BF)


def d_hidden_near_kernel(place_ref, *refs):
    for dl in range(2):
        for i in range(8):
            part = d_hidden_block(place_ref, refs, dl, i)
            refs[6 + i // 2][i % 2, dl] = (part + refs[5][i, dl].astype(F32)).astype(BF)


def d_hidden_away(place, dq, weights):
    work = cost(1024 * 2048 * 512, 5 << 20)
    outs = [((8, 2, T, T), BF)]
    return in_vmem(d_hidden_away_kernel, "d_hidden_away", work, outs, place, *dq, weights, room=56)[0]


def d_hidden_near(place, dq, weights, away):
    work = cost(1024 * 2048 * 512, 7 << 20)
    outs = [((2, 2, T, T), BF)] * 4
    return in_vmem(d_hidden_near_kernel, "d_hidden_near", work, outs, place, *dq, weights, away)


def d_weight_kernel(place_ref, *refs):
    own, other, dqs, out_ref = refs[:4], refs[4:8], refs[8:12], refs[12]
    dq = jnp.concatenate(
        [
            jnp.concatenate(
                [
                    ref[pl.ds(pl.multiple_of(place_ref[8 + j] * T, T), T), :]
                    for ref in dqs
                ],
                axis=1,
            )
            for j in range(4)
        ],
        axis=0,
    )
    for i in range(8):
        h = jnp.concatenate(
            [feature_block(tokens, i, dl) for tokens in (own, other) for dl in range(2)], axis=0
        )
        out_ref[place_ref[i]] = mm(h, dq, ((0,), (0,))).astype(BF)


def d_weight_part(place, own, other, dq):
    work = cost(2 * 1024 * 2048 * 512, 7 << 20)
    outs = [((NZ, T, 4 * DH), BF)]
    return in_vmem(d_weight_kernel, "d_weight_part", work, outs, place, *own, *other, *dq)[0]


def attended_kernel(place_ref, own_ref, core_ref, y_ref, *outs):
    for k, ref in enumerate((own_ref, core_ref.at[0], y_ref.at[0], core_ref.at[1])):
        at = pl.multiple_of(place_ref[12 + k] * DH, DH)
        for j in range(3):
            outs[j][:, pl.ds(at, DH)] = ref[j]


def last_kernel(place_ref, *refs):
    for k in range(4):
        at = place_ref[16 + k]
        for co in range(2):
            first = pl.multiple_of((at + co * 2) * DH, DH)
            refs[8][:, pl.ds(first, DH)] = refs[k][:, co * DH : (co + 1) * DH]
    for dy in range(2):
        row = pl.multiple_of(place_ref[20 + dy] * DH, DH)
        for dc in range(2):
            for dl in range(2):
                at = pl.multiple_of(place_ref[12 + dl * 2 + dc] * DH, DH)
                refs[9][pl.ds(row, DH), pl.ds(at, DH)] = refs[4 + dy * 2 + dc][
                    :, dl * DH : (dl + 1) * DH
                ]


def attend_kernel(
    place_ref, q0_ref, q1_ref, q2_ref, q3_ref, p0_ref, p1_ref, p2_ref, prev0_ref, prev1_ref,
    out_ref, dq_ref, dkv_ref, dprev_ref, k_ref, v_ref, g_ref, o_ref, dk_ref, dv_ref,
):
    tokens = [pl.multiple_of(place_ref[12 + k] * T, T) for k in range(4)]
    for half, ref in enumerate((prev0_ref, prev1_ref)):
        k_ref[half * T : (half + 1) * T] = ref[0]
        v_ref[half * T : (half + 1) * T] = ref[1]
    for row, ref in zip(tokens, (p0_ref, p1_ref.at[0], p2_ref.at[0], p2_ref.at[1])):
        k_ref[pl.ds(W + row, T), :] = ref[0]
        v_ref[pl.ds(W + row, T), :] = ref[1]
        g_ref[pl.ds(row, T), :] = ref[2]
    dk_ref[...] = jnp.zeros_like(dk_ref)
    dv_ref[...] = jnp.zeros_like(dv_ref)
    inside = place_ref[22] == 0
    rows = lax.broadcasted_iota(jnp.int32, (T, T), 0)
    cols = lax.broadcasted_iota(jnp.int32, (T, T), 1)
    old = cols > rows
    for i in range(4):
        at = slice(i * T, (i + 1) * T)
        window = slice(i * T, i * T + W + T)
        q = (
            q0_ref[at].astype(F32) + q1_ref[at].astype(F32)
            + q2_ref[at].astype(F32) + q3_ref[at].astype(F32)
        ).astype(BF)
        g = g_ref[at]
        k = k_ref[window]
        v = v_ref[window]
        s = mm(q, k, ((1,), (1,)))
        sa, sb, sc = s[:, :T], s[:, T : 2 * T], s[:, 2 * T :]
        if i < 2:
            sa = jnp.where(inside, sa, -1e30)
        if i < 1:
            sb = jnp.where(inside, sb, -1e30)
        sm = jnp.where(old, sa, sc)
        top = jnp.max(jnp.maximum(sm, sb), axis=1, keepdims=True)
        em = jnp.exp2((sm - top) * (SCALE * LOG2E))
        eb = jnp.exp2((sb - top) * (SCALE * LOG2E))
        inv = 1.0 / jnp.sum(em + eb, axis=1, keepdims=True)
        pm = em * inv
        pb = eb * inv
        prob = jnp.concatenate(
            [
                jnp.where(old, pm, 0.0).astype(BF),
                pb.astype(BF),
                jnp.where(old, 0.0, pm).astype(BF),
            ],
            axis=1,
        )
        o_ref[at] = mm(prob, v, ((1,), (0,))).astype(BF)
        dp = mm(g, v, ((1,), (1,)))
        dpm = jnp.where(old, dp[:, :T], dp[:, 2 * T :])
        dpb = dp[:, T : 2 * T]
        delta = jnp.sum(pm * dpm + pb * dpb, axis=1, keepdims=True)
        dsm = pm * (dpm - delta) * SCALE
        dsb = pb * (dpb - delta) * SCALE
        ds = jnp.concatenate(
            [
                jnp.where(old, dsm, 0.0).astype(BF),
                dsb.astype(BF),
                jnp.where(old, 0.0, dsm).astype(BF),
            ],
            axis=1,
        )
        dq_ref[at] = mm(ds, k, ((1,), (0,))).astype(BF)
        dk_ref[window] += mm(ds, q, ((0,), (0,)))
        dv_ref[window] += mm(prob, g, ((0,), (0,)))
    for half in range(2):
        dprev_ref[half, 0] = dk_ref[half * T : (half + 1) * T].astype(BF)
        dprev_ref[half, 1] = dv_ref[half * T : (half + 1) * T].astype(BF)
    for k, row in enumerate(tokens):
        out_ref[k] = o_ref[pl.ds(row, T), :]
        dkv_ref[k, 0] = dk_ref[pl.ds(W + row, T), :]
        dkv_ref[k, 1] = dv_ref[pl.ds(W + row, T), :]


def attend(place, parts, pieces, prev):
    vm = pl.BlockSpec(memory_space=pltpu.VMEM)
    n = 4 * T
    return pl.pallas_call(
        attend_kernel,
        in_specs=[pl.BlockSpec(memory_space=pltpu.SMEM)] + [vm] * 9,
        out_specs=[vm] * 4,
        out_shape=[
            jax.ShapeDtypeStruct((4, T, DH), BF),
            jax.ShapeDtypeStruct((n, DH), BF),
            jax.ShapeDtypeStruct((4, 2, T, DH), F32),
            jax.ShapeDtypeStruct((2, 2, T, DH), BF),
        ],
        scratch_shapes=[
            pltpu.VMEM((W + n, DH), BF),
            pltpu.VMEM((W + n, DH), BF),
            pltpu.VMEM((n, DH), BF),
            pltpu.VMEM((n, DH), BF),
            pltpu.VMEM((W + n, DH), F32),
            pltpu.VMEM((W + n, DH), F32),
        ],
        compiler_params=params(56),
        cost_estimate=cost(12 * n * 768 * DH, 5 << 20, n * W),
        name="attend",
    )(place, *parts, *pieces, *prev)


def tie(*groups):
    flat = iter(lax.optimization_barrier([a for group in groups for a in group]))
    return [[next(flat) for _ in group] for group in groups]


def after(group, *others):
    return tie(group, others)[0]


def per_device(hidden, weight, keys, values, d_attended):
    z, yl, co, yh, x = (lax.axis_index(a) for a in AXES)
    quad = [(a, b) for a in range(2) for b in range(2)]
    blocks = [(yh ^ dy) * NX + (x - dx) % NX for dx in range(NX) for dy in range(2)]
    rows = [(yl ^ dl) * 2 + (co ^ dc) for dc, dl in quad]
    heads = [(yl ^ dl) * 2 + (co ^ dc) for dl, dc in quad]
    lanes = [(yl ^ dl) * 4 + (yh ^ dy) for dy, dl in quad]
    tail = heads + lanes + [yh, 1 - yh, (z % SEQ_Z == 0).astype(jnp.int32)]
    place = jnp.stack(blocks + rows + tail).astype(jnp.int32)
    place_other = jnp.stack(blocks + rows[2:] + rows[:2] + tail).astype(jnp.int32)

    def weight_piece(dc, dy):
        half = lax.dynamic_slice_in_dim(weight, (yh ^ dy) * DH, DH, 0)
        return jnp.concatenate(
            [
                lax.dynamic_slice_in_dim(half, ((yl ^ dl) * 2 + (co ^ dc)) * DH, DH, 1)
                for dl in range(2)
            ],
            axis=1,
        )

    kvd = [
        jnp.stack(
            [lax.dynamic_slice_in_dim(a, heads[k] * DH, DH, 1) for a in (keys, values, d_attended)]
        )
        for k in range(4)
    ]

    sent = [weight_piece(dc, dy) for dc, dy in quad]
    got = [sent[0], move(sent[1], yh=1), move(sent[2], co=1), move(sent[3], co=1, yh=1)]
    mine = jnp.concatenate(got[:2], axis=1)
    theirs = jnp.concatenate(got[2:], axis=1)
    shard = jnp.concatenate(
        [jnp.where(co == 0, mine, theirs), jnp.where(co == 0, theirs, mine)], axis=0
    )

    def hidden_piece(dy, dl):
        part = lax.dynamic_slice_in_dim(hidden, (yl ^ dl) * 2 * T, 2 * T, 1)
        part = part.reshape(T, 2, 2, DH)
        return lax.dynamic_index_in_dim(part, yh ^ dy, 2, keepdims=False).reshape(T, T)

    mixed = [hidden_piece(dy, dl) for dy, dl in quad]
    mixed = [mixed[0]] + [move(mixed[k], yh=quad[k][0], yl=quad[k][1]) for k in (1, 2, 3)]
    mixed = jnp.stack(mixed).reshape(2, 2, T, T)

    own = [move(mixed, dx=dx) if dx else mixed for dx in range(NX)]
    other = [move(block, co=1) for block in own]
    kvd = after(kvd, mixed)
    swapped = move(jnp.stack([kvd[1], kvd[3]]), co=1)
    pieces = [kvd[0], swapped, move(jnp.stack([kvd[2], swapped[1]]), yl=1)]
    weights = lax.all_gather(shard, "z", axis=0, tiled=False)
    own, other, (weights,) = tie(own, other, (weights,))

    parts = query_part(place, own, other, weights)
    pieces = after(pieces, *parts)
    low = jnp.where(yl == 1, jnp.stack([pieces[0][:2], pieces[1][0, :2]]), pieces[2][:, :2])
    prev = [move(lax.dynamic_index_in_dim(low, co ^ k, 0, keepdims=False), dz=1) for k in range(2)]
    parts = [parts[0]] + [move(parts[k], yh=k // 2, yl=k % 2) for k in (3, 2, 1)]
    attended, dq, dkv, dprev = attend(place, parts, pieces, prev)
    dq = [dq] + [move(dq, yh=k // 2, yl=k % 2) for k in range(1, 4)]

    late = [move(dprev[half], dz=-1) for half in range(2)]
    dq, late = tie(dq, late)
    late = jnp.stack(late)

    sums = d_weight_part(place, own, other, dq)
    shard = lax.psum_scatter(sums.reshape(NZ * T, 4 * DH), "z", scatter_dimension=0, tiled=True)
    away = move(d_hidden_away(place_other, dq, weights), co=1)
    near = d_hidden_near(place, dq, weights, away)
    line = [near[0]] + [move(near[dx], dx=-dx) for dx in range(1, NX)]

    outs = []
    for k, (dl, dc) in enumerate(quad):
        half = lax.dynamic_index_in_dim(late, co ^ dc, 0, keepdims=False).astype(F32)
        grads = dkv[k] + jnp.where((yl ^ dl) == 1, half, 0.0)
        outs.append(jnp.concatenate([attended[k][None], grads.astype(BF)], axis=0))

    crossed = move(jnp.stack(outs[2:]), yl=1)
    outs = [outs[0], move(jnp.stack([outs[1], crossed[1]]), co=1), crossed]
    result = in_vmem(
        attended_kernel, "attended_last", cost(0, 1 << 20), [((T, 4 * DH), BF)] * 3, place, *outs
    )

    def weight_back(dc, dy):
        block = lax.dynamic_slice_in_dim(shard, (co ^ dc) * DH, DH, 0)
        return block[:, dy * T : (dy + 1) * T]

    ends = [weight_back(dc, dy) for dy, dc in quad]
    line = after(line, *ends)
    ends = [move(ends[k], yh=quad[k][0], co=quad[k][1]) if k else ends[0] for k in range(4)]
    line = sum(block.astype(F32) for block in line).astype(BF)
    back = [line[dy, dl] for dy, dl in quad]
    back = [back[0]] + [move(back[k], yh=quad[k][0], yl=quad[k][1]) for k in (1, 2, 3)]
    back += ends
    d_hidden, d_weight = in_vmem(
        last_kernel, "last", cost(0, 1 << 20), [((T, 8 * DH), BF), ((T, 4 * DH), BF)], place, *back
    )

    return result[0], d_hidden, d_weight, result[1], result[2]


def solution(mesh):
    grid = Mesh(mesh.devices.reshape(SIZES), AXES)
    spec = P(("z", "yl", "co"), ("yh", "x"))
    return jax.shard_map(
        per_device, mesh=grid, in_specs=(spec,) * 5, out_specs=(spec,) * 5, check_vma=False
    )
```

```python
import jax
import jax.numpy as jnp
from jax import lax
from jax.experimental import pallas as pl
from jax.experimental.pallas import tpu as pltpu
from jax.sharding import Mesh, PartitionSpec as P

DH = 128
W = 512
SEQ_Z = 4
AXES = ("z", "yl", "co", "yh", "x")
SIZES = (8, 2, 2, 2, 4)
NZ, NX = 8, 4
T = 256
SCALE = 1.0 / DH**0.5
LOG2E = 1.4426950408889634
BF = jnp.bfloat16
F32 = jnp.float32


def route(target):
    pairs = []
    for i in range(256):
        rest, place = i, []
        for size in SIZES[::-1]:
            place.append(rest % size)
            rest //= size
        there = target(*place[::-1])
        j = 0
        for size, c in zip(SIZES, there):
            j = j * size + c % size
        pairs.append((i, j))
    return pairs


def move(block, dz=0, yl=0, co=0, yh=0, dx=0):
    pairs = route(lambda z, a, b, c, x: (z + dz, a ^ yl, b ^ co, c ^ yh, x + dx))
    return lax.ppermute(block, AXES, pairs)


def params(mebibytes=20):
    return pltpu.CompilerParams(vmem_limit_bytes=mebibytes * 1024 * 1024)


def cost(flops, bytes_accessed, exps=0):
    return pl.CostEstimate(flops=flops, bytes_accessed=bytes_accessed, transcendentals=exps)


def mm(a, b, dims):
    return lax.dot_general(a, b, (dims, ((), ())), preferred_element_type=F32)


def feature_block(tokens, i, dl):
    return tokens[i // 2][i % 2, dl]


def query_kernel(place_ref, *refs):
    own, other, w_ref, outs = refs[:4], refs[4:8], refs[8], refs[9:13]
    w = jnp.concatenate([w_ref[place_ref[i]] for i in range(8)], axis=0)
    for dc, tokens in enumerate((own, other)):
        for dl in range(2):
            h = jnp.concatenate([feature_block(tokens, i, dl) for i in range(8)], axis=1)
            part = mm(h, w, ((1,), (0,))).astype(BF)
            row = pl.multiple_of(place_ref[8 + dc * 2 + dl] * T, T)
            for k in range(4):
                outs[k][pl.ds(row, T), :] = part[:, k * DH : (k + 1) * DH]


def in_vmem(kernel, name, work, outs, *args, room=20):
    vm = pl.BlockSpec(memory_space=pltpu.VMEM)
    return pl.pallas_call(
        kernel,
        in_specs=[pl.BlockSpec(memory_space=pltpu.SMEM)] + [vm] * (len(args) - 1),
        out_specs=[vm] * len(outs),
        out_shape=[jax.ShapeDtypeStruct(shape, kind) for shape, kind in outs],
        compiler_params=params(room),
        cost_estimate=work,
        name=name,
    )(*args)


def query_part(place, own, other, weights):
    work = cost(2 * 1024 * 2048 * 512, 7 << 20)
    outs = [((4 * T, DH), BF)] * 4
    return in_vmem(query_kernel, "query_part", work, outs, place, *own, *other, weights, room=20)


def d_hidden_block(place_ref, refs, dl, i):
    row = pl.multiple_of(place_ref[8 + dl] * T, T)
    dq = jnp.concatenate([refs[k][pl.ds(row, T), :] for k in range(4)], axis=1)
    return mm(dq, refs[4][place_ref[i]], ((1,), (1,)))


def d_hidden_away_kernel(place_ref, *refs):
    for dl in range(2):
        for i in range(8):
            refs[5][i, dl] = d_hidden_block(place_ref, refs, dl, i).astype(BF)


def d_hidden_near_kernel(place_ref, *refs):
    for dl in range(2):
        for i in range(8):
            part = d_hidden_block(place_ref, refs, dl, i)
            refs[6 + i // 2][i % 2, dl] = (part + refs[5][i, dl].astype(F32)).astype(BF)


def d_hidden_away(place, dq, weights):
    work = cost(1024 * 2048 * 512, 5 << 20)
    outs = [((8, 2, T, T), BF)]
    return in_vmem(d_hidden_away_kernel, "d_hidden_away", work, outs, place, *dq, weights, room=20)[0]


def d_hidden_near(place, dq, weights, away):
    work = cost(1024 * 2048 * 512, 7 << 20)
    outs = [((2, 2, T, T), BF)] * 4
    return in_vmem(d_hidden_near_kernel, "d_hidden_near", work, outs, place, *dq, weights, away)


def d_weight_kernel(place_ref, *refs):
    own, other, dqs, out_ref = refs[:4], refs[4:8], refs[8:12], refs[12]
    dq = jnp.concatenate(
        [
            jnp.concatenate(
                [
                    ref[pl.ds(pl.multiple_of(place_ref[8 + j] * T, T), T), :]
                    for ref in dqs
                ],
                axis=1,
            )
            for j in range(4)
        ],
        axis=0,
    )
    for i in range(8):
        h = jnp.concatenate(
            [feature_block(tokens, i, dl) for tokens in (own, other) for dl in range(2)], axis=0
        )
        out_ref[place_ref[i]] = mm(h, dq, ((0,), (0,))).astype(BF)


def d_weight_part(place, own, other, dq):
    work = cost(2 * 1024 * 2048 * 512, 7 << 20)
    outs = [((NZ, T, 4 * DH), BF)]
    return in_vmem(d_weight_kernel, "d_weight_part", work, outs, place, *own, *other, *dq)[0]


def attended_kernel(place_ref, own_ref, core_ref, y_ref, *outs):
    for k, ref in enumerate((own_ref, core_ref.at[0], y_ref.at[0], core_ref.at[1])):
        at = pl.multiple_of(place_ref[12 + k] * DH, DH)
        for j in range(3):
            outs[j][:, pl.ds(at, DH)] = ref[j]


def last_kernel(place_ref, *refs):
    for k in range(4):
        at = place_ref[16 + k]
        for co in range(2):
            first = pl.multiple_of((at + co * 2) * DH, DH)
            refs[8][:, pl.ds(first, DH)] = refs[k][:, co * DH : (co + 1) * DH]
    for dy in range(2):
        row = pl.multiple_of(place_ref[20 + dy] * DH, DH)
        for dc in range(2):
            for dl in range(2):
                at = pl.multiple_of(place_ref[12 + dl * 2 + dc] * DH, DH)
                refs[9][pl.ds(row, DH), pl.ds(at, DH)] = refs[4 + dy * 2 + dc][
                    :, dl * DH : (dl + 1) * DH
                ]


def attend_kernel(
    place_ref, q0_ref, q1_ref, q2_ref, q3_ref, p0_ref, p1_ref, p2_ref, prev0_ref, prev1_ref,
    out_ref, dq_ref, dkv_ref, dprev_ref, k_ref, v_ref, g_ref, o_ref, dk_ref, dv_ref,
):
    tokens = [pl.multiple_of(place_ref[12 + k] * T, T) for k in range(4)]
    for half, ref in enumerate((prev0_ref, prev1_ref)):
        k_ref[half * T : (half + 1) * T] = ref[0]
        v_ref[half * T : (half + 1) * T] = ref[1]
    for row, ref in zip(tokens, (p0_ref, p1_ref.at[0], p2_ref.at[0], p2_ref.at[1])):
        k_ref[pl.ds(W + row, T), :] = ref[0]
        v_ref[pl.ds(W + row, T), :] = ref[1]
        g_ref[pl.ds(row, T), :] = ref[2]
    dk_ref[...] = jnp.zeros_like(dk_ref)
    dv_ref[...] = jnp.zeros_like(dv_ref)
    inside = place_ref[22] == 0
    rows = lax.broadcasted_iota(jnp.int32, (T, T), 0)
    cols = lax.broadcasted_iota(jnp.int32, (T, T), 1)
    old = cols > rows
    for i in range(4):
        at = slice(i * T, (i + 1) * T)
        window = slice(i * T, i * T + W + T)
        q = (
            q0_ref[at].astype(F32) + q1_ref[at].astype(F32)
            + q2_ref[at].astype(F32) + q3_ref[at].astype(F32)
        ).astype(BF)
        g = g_ref[at]
        k = k_ref[window]
        v = v_ref[window]
        s = mm(q, k, ((1,), (1,)))
        sa, sb, sc = s[:, :T], s[:, T : 2 * T], s[:, 2 * T :]
        if i < 2:
            sa = jnp.where(inside, sa, -1e30)
        if i < 1:
            sb = jnp.where(inside, sb, -1e30)
        sm = jnp.where(old, sa, sc)
        top = jnp.max(jnp.maximum(sm, sb), axis=1, keepdims=True)
        em = jnp.exp2((sm - top) * (SCALE * LOG2E))
        eb = jnp.exp2((sb - top) * (SCALE * LOG2E))
        inv = 1.0 / jnp.sum(em + eb, axis=1, keepdims=True)
        pm = em * inv
        pb = eb * inv
        prob = jnp.concatenate(
            [
                jnp.where(old, pm, 0.0).astype(BF),
                pb.astype(BF),
                jnp.where(old, 0.0, pm).astype(BF),
            ],
            axis=1,
        )
        o_ref[at] = mm(prob, v, ((1,), (0,))).astype(BF)
        dp = mm(g, v, ((1,), (1,)))
        dpm = jnp.where(old, dp[:, :T], dp[:, 2 * T :])
        dpb = dp[:, T : 2 * T]
        delta = jnp.sum(pm * dpm + pb * dpb, axis=1, keepdims=True)
        dsm = pm * (dpm - delta) * SCALE
        dsb = pb * (dpb - delta) * SCALE
        ds = jnp.concatenate(
            [
                jnp.where(old, dsm, 0.0).astype(BF),
                dsb.astype(BF),
                jnp.where(old, 0.0, dsm).astype(BF),
            ],
            axis=1,
        )
        dq_ref[at] = mm(ds, k, ((1,), (0,))).astype(BF)
        dk_ref[window] += mm(ds, q, ((0,), (0,)))
        dv_ref[window] += mm(prob, g, ((0,), (0,)))
    for half in range(2):
        dprev_ref[half, 0] = dk_ref[half * T : (half + 1) * T].astype(BF)
        dprev_ref[half, 1] = dv_ref[half * T : (half + 1) * T].astype(BF)
    for k, row in enumerate(tokens):
        out_ref[k] = o_ref[pl.ds(row, T), :]
        dkv_ref[k, 0] = dk_ref[pl.ds(W + row, T), :]
        dkv_ref[k, 1] = dv_ref[pl.ds(W + row, T), :]


def attend(place, parts, pieces, prev):
    vm = pl.BlockSpec(memory_space=pltpu.VMEM)
    n = 4 * T
    return pl.pallas_call(
        attend_kernel,
        in_specs=[pl.BlockSpec(memory_space=pltpu.SMEM)] + [vm] * 9,
        out_specs=[vm] * 4,
        out_shape=[
            jax.ShapeDtypeStruct((4, T, DH), BF),
            jax.ShapeDtypeStruct((n, DH), BF),
            jax.ShapeDtypeStruct((4, 2, T, DH), F32),
            jax.ShapeDtypeStruct((2, 2, T, DH), BF),
        ],
        scratch_shapes=[
            pltpu.VMEM((W + n, DH), BF),
            pltpu.VMEM((W + n, DH), BF),
            pltpu.VMEM((n, DH), BF),
            pltpu.VMEM((n, DH), BF),
            pltpu.VMEM((W + n, DH), F32),
            pltpu.VMEM((W + n, DH), F32),
        ],
        compiler_params=params(20),
        cost_estimate=cost(12 * n * 768 * DH, 5 << 20, n * W),
        name="attend",
    )(place, *parts, *pieces, *prev)


def tie(*groups):
    flat = iter(lax.optimization_barrier([a for group in groups for a in group]))
    return [[next(flat) for _ in group] for group in groups]


def after(group, *others):
    return tie(group, others)[0]


def per_device(hidden, weight, keys, values, d_attended):
    z, yl, co, yh, x = (lax.axis_index(a) for a in AXES)
    quad = [(a, b) for a in range(2) for b in range(2)]
    blocks = [(yh ^ dy) * NX + (x - dx) % NX for dx in range(NX) for dy in range(2)]
    rows = [(yl ^ dl) * 2 + (co ^ dc) for dc, dl in quad]
    heads = [(yl ^ dl) * 2 + (co ^ dc) for dl, dc in quad]
    lanes = [(yl ^ dl) * 4 + (yh ^ dy) for dy, dl in quad]
    tail = heads + lanes + [yh, 1 - yh, (z % SEQ_Z == 0).astype(jnp.int32)]
    place = jnp.stack(blocks + rows + tail).astype(jnp.int32)
    place_other = jnp.stack(blocks + rows[2:] + rows[:2] + tail).astype(jnp.int32)

    def weight_piece(dc, dy):
        half = lax.dynamic_slice_in_dim(weight, (yh ^ dy) * DH, DH, 0)
        return jnp.concatenate(
            [
                lax.dynamic_slice_in_dim(half, ((yl ^ dl) * 2 + (co ^ dc)) * DH, DH, 1)
                for dl in range(2)
            ],
            axis=1,
        )

    kvd = [
        jnp.stack(
            [lax.dynamic_slice_in_dim(a, heads[k] * DH, DH, 1) for a in (keys, values, d_attended)]
        )
        for k in range(4)
    ]

    sent = [weight_piece(dc, dy) for dc, dy in quad]
    got = [sent[0], move(sent[1], yh=1), move(sent[2], co=1), move(sent[3], co=1, yh=1)]
    mine = jnp.concatenate(got[:2], axis=1)
    theirs = jnp.concatenate(got[2:], axis=1)
    shard = jnp.concatenate(
        [jnp.where(co == 0, mine, theirs), jnp.where(co == 0, theirs, mine)], axis=0
    )

    def hidden_piece(dy, dl):
        part = lax.dynamic_slice_in_dim(hidden, (yl ^ dl) * 2 * T, 2 * T, 1)
        part = part.reshape(T, 2, 2, DH)
        return lax.dynamic_index_in_dim(part, yh ^ dy, 2, keepdims=False).reshape(T, T)

    mixed = [hidden_piece(dy, dl) for dy, dl in quad]
    mixed = [mixed[0]] + [move(mixed[k], yh=quad[k][0], yl=quad[k][1]) for k in (1, 2, 3)]
    mixed = jnp.stack(mixed).reshape(2, 2, T, T)

    own = [move(mixed, dx=dx) if dx else mixed for dx in range(NX)]
    other = [move(block, co=1) for block in own]
    kvd = after(kvd, mixed)
    swapped = move(jnp.stack([kvd[1], kvd[3]]), co=1)
    pieces = [kvd[0], swapped, move(jnp.stack([kvd[2], swapped[1]]), yl=1)]
    weights = lax.all_gather(shard, "z", axis=0, tiled=False)
    own, other, (weights,) = tie(own, other, (weights,))

    parts = query_part(place, own, other, weights)
    pieces = after(pieces, *parts)
    low = jnp.where(yl == 1, jnp.stack([pieces[0][:2], pieces[1][0, :2]]), pieces[2][:, :2])
    prev = [move(lax.dynamic_index_in_dim(low, co ^ k, 0, keepdims=False), dz=1) for k in range(2)]
    parts = [parts[0]] + [move(parts[k], yh=k // 2, yl=k % 2) for k in (3, 2, 1)]
    attended, dq, dkv, dprev = attend(place, parts, pieces, prev)
    dq = [dq] + [move(dq, yh=k // 2, yl=k % 2) for k in range(1, 4)]

    late = [move(dprev[half], dz=-1) for half in range(2)]
    dq, late = tie(dq, late)
    late = jnp.stack(late)

    sums = d_weight_part(place, own, other, dq)
    shard = lax.psum_scatter(sums.reshape(NZ * T, 4 * DH), "z", scatter_dimension=0, tiled=True)
    away = move(d_hidden_away(place_other, dq, weights), co=1)
    near = d_hidden_near(place, dq, weights, away)
    line = [near[0]] + [move(near[dx], dx=-dx) for dx in range(1, NX)]

    outs = []
    for k, (dl, dc) in enumerate(quad):
        half = lax.dynamic_index_in_dim(late, co ^ dc, 0, keepdims=False).astype(F32)
        grads = dkv[k] + jnp.where((yl ^ dl) == 1, half, 0.0)
        outs.append(jnp.concatenate([attended[k][None], grads.astype(BF)], axis=0))

    crossed = move(jnp.stack(outs[2:]), yl=1)
    outs = [outs[0], move(jnp.stack([outs[1], crossed[1]]), co=1), crossed]
    result = in_vmem(
        attended_kernel, "attended_last", cost(0, 1 << 20), [((T, 4 * DH), BF)] * 3, place, *outs
    )

    def weight_back(dc, dy):
        block = lax.dynamic_slice_in_dim(shard, (co ^ dc) * DH, DH, 0)
        return block[:, dy * T : (dy + 1) * T]

    ends = [weight_back(dc, dy) for dy, dc in quad]
    line = after(line, *ends)
    ends = [move(ends[k], yh=quad[k][0], co=quad[k][1]) if k else ends[0] for k in range(4)]
    line = sum(block.astype(F32) for block in line).astype(BF)
    back = [line[dy, dl] for dy, dl in quad]
    back = [back[0]] + [move(back[k], yh=quad[k][0], yl=quad[k][1]) for k in (1, 2, 3)]
    back += ends
    d_hidden, d_weight = in_vmem(
        last_kernel, "last", cost(0, 1 << 20), [((T, 8 * DH), BF), ((T, 4 * DH), BF)], place, *back
    )

    return result[0], d_hidden, d_weight, result[1], result[2]


def solution(mesh):
    grid = Mesh(mesh.devices.reshape(SIZES), AXES)
    spec = P(("z", "yl", "co"), ("yh", "x"))
    return jax.shard_map(
        per_device, mesh=grid, in_specs=(spec,) * 5, out_specs=(spec,) * 5, check_vma=False
    )
```

```python
import jax
import jax.numpy as jnp
from jax import lax
from jax.experimental import pallas as pl
from jax.experimental.pallas import tpu as pltpu
from jax.sharding import Mesh, PartitionSpec as P

DH = 128
W = 512
SEQ_Z = 4
AXES = ("z", "yl", "co", "yh", "x")
SIZES = (8, 2, 2, 2, 4)
NZ, NX = 8, 4
T = 256
SCALE = 1.0 / DH**0.5
LOG2E = 1.4426950408889634
BF = jnp.bfloat16
F32 = jnp.float32


def route(target):
    pairs = []
    for i in range(256):
        rest, place = i, []
        for size in SIZES[::-1]:
            place.append(rest % size)
            rest //= size
        there = target(*place[::-1])
        j = 0
        for size, c in zip(SIZES, there):
            j = j * size + c % size
        pairs.append((i, j))
    return pairs


def move(block, dz=0, yl=0, co=0, yh=0, dx=0):
    pairs = route(lambda z, a, b, c, x: (z + dz, a ^ yl, b ^ co, c ^ yh, x + dx))
    return lax.ppermute(block, AXES, pairs)


def params(mebibytes=20):
    return pltpu.CompilerParams(vmem_limit_bytes=mebibytes * 1024 * 1024)


def cost(flops, bytes_accessed, exps=0):
    return pl.CostEstimate(flops=flops, bytes_accessed=bytes_accessed, transcendentals=exps)


def mm(a, b, dims):
    return lax.dot_general(a, b, (dims, ((), ())), preferred_element_type=F32)


def feature_block(tokens, i, dl):
    return tokens[i // 2][i % 2, dl]


def query_kernel(place_ref, *refs):
    own, other, w_ref, outs = refs[:4], refs[4:8], refs[8], refs[9:13]
    w = jnp.concatenate([w_ref[place_ref[i]] for i in range(8)], axis=0)
    for dc, tokens in enumerate((own, other)):
        for dl in range(2):
            h = jnp.concatenate([feature_block(tokens, i, dl) for i in range(8)], axis=1)
            part = mm(h, w, ((1,), (0,))).astype(BF)
            row = pl.multiple_of(place_ref[8 + dc * 2 + dl] * T, T)
            for k in range(4):
                outs[k][pl.ds(row, T), :] = part[:, k * DH : (k + 1) * DH]


def in_vmem(kernel, name, work, outs, *args, room=20):
    vm = pl.BlockSpec(memory_space=pltpu.VMEM)
    return pl.pallas_call(
        kernel,
        in_specs=[pl.BlockSpec(memory_space=pltpu.SMEM)] + [vm] * (len(args) - 1),
        out_specs=[vm] * len(outs),
        out_shape=[jax.ShapeDtypeStruct(shape, kind) for shape, kind in outs],
        compiler_params=params(room),
        cost_estimate=work,
        name=name,
    )(*args)


def query_part(place, own, other, weights):
    work = cost(2 * 1024 * 2048 * 512, 7 << 20)
    outs = [((4 * T, DH), BF)] * 4
    return in_vmem(query_kernel, "query_part", work, outs, place, *own, *other, weights, room=20)


def d_hidden_block(place_ref, refs, dl, i):
    row = pl.multiple_of(place_ref[8 + dl] * T, T)
    dq = jnp.concatenate([refs[k][pl.ds(row, T), :] for k in range(4)], axis=1)
    return mm(dq, refs[4][place_ref[i]], ((1,), (1,)))


def d_hidden_near_kernel(place_ref, *refs):
    for dl in range(2):
        for i in range(8):
            part = d_hidden_block(place_ref, refs, dl, i)
            refs[6 + i // 2][i % 2, dl] = (part + refs[5][i, dl].astype(F32)).astype(BF)


def d_hidden_near(place, dq, weights, away):
    work = cost(1024 * 2048 * 512, 7 << 20)
    outs = [((2, 2, T, T), BF)] * 4
    return in_vmem(d_hidden_near_kernel, "d_hidden_near", work, outs, place, *dq, weights, away)


def d_weight_kernel(place_ref, *refs):
    own, other, dqs, out_ref, away_ref = refs[:4], refs[4:8], refs[8:12], refs[13], refs[14]
    dq = jnp.concatenate(
        [
            jnp.concatenate(
                [
                    ref[pl.ds(pl.multiple_of(place_ref[8 + j] * T, T), T), :]
                    for ref in dqs
                ],
                axis=1,
            )
            for j in range(4)
        ],
        axis=0,
    )
    for i in range(8):
        h = jnp.concatenate(
            [feature_block(tokens, i, dl) for tokens in (own, other) for dl in range(2)], axis=0
        )
        out_ref[place_ref[i]] = mm(h, dq, ((0,), (0,))).astype(BF)
    for dl in range(2):
        for i in range(8):
            away_ref[i, dl] = d_hidden_block(place_ref, refs[8:13], dl + 2, i).astype(BF)


def d_weight_part(place, own, other, dq, weights):
    work = cost(3 * 1024 * 2048 * 512, 11 << 20)
    outs = [((NZ, T, 4 * DH), BF), ((8, 2, T, T), BF)]
    return in_vmem(
        d_weight_kernel, "d_weight_part", work, outs, place, *own, *other, *dq, weights
    )


def attended_kernel(place_ref, own_ref, core_ref, y_ref, *outs):
    for k, ref in enumerate((own_ref, core_ref.at[0], y_ref.at[0], core_ref.at[1])):
        at = pl.multiple_of(place_ref[12 + k] * DH, DH)
        for j in range(3):
            outs[j][:, pl.ds(at, DH)] = ref[j]


def last_kernel(place_ref, *refs):
    for k in range(4):
        at = place_ref[16 + k]
        for co in range(2):
            first = pl.multiple_of((at + co * 2) * DH, DH)
            refs[8][:, pl.ds(first, DH)] = refs[k][:, co * DH : (co + 1) * DH]
    for dy in range(2):
        row = pl.multiple_of(place_ref[20 + dy] * DH, DH)
        for dc in range(2):
            for dl in range(2):
                at = pl.multiple_of(place_ref[12 + dl * 2 + dc] * DH, DH)
                refs[9][pl.ds(row, DH), pl.ds(at, DH)] = refs[4 + dy * 2 + dc][
                    :, dl * DH : (dl + 1) * DH
                ]


def attend_kernel(
    place_ref, q0_ref, q1_ref, q2_ref, q3_ref, p0_ref, p1_ref, p2_ref, prev0_ref, prev1_ref,
    out_ref, dq_ref, dkv_ref, dprev_ref, k_ref, v_ref, g_ref, o_ref, dk_ref, dv_ref,
):
    tokens = [pl.multiple_of(place_ref[12 + k] * T, T) for k in range(4)]
    for half, ref in enumerate((prev0_ref, prev1_ref)):
        k_ref[half * T : (half + 1) * T] = ref[0]
        v_ref[half * T : (half + 1) * T] = ref[1]
    for row, ref in zip(tokens, (p0_ref, p1_ref.at[0], p2_ref.at[0], p2_ref.at[1])):
        k_ref[pl.ds(W + row, T), :] = ref[0]
        v_ref[pl.ds(W + row, T), :] = ref[1]
        g_ref[pl.ds(row, T), :] = ref[2]
    dk_ref[...] = jnp.zeros_like(dk_ref)
    dv_ref[...] = jnp.zeros_like(dv_ref)
    inside = place_ref[22] == 0
    rows = lax.broadcasted_iota(jnp.int32, (T, T), 0)
    cols = lax.broadcasted_iota(jnp.int32, (T, T), 1)
    old = cols > rows
    for i in range(4):
        at = slice(i * T, (i + 1) * T)
        window = slice(i * T, i * T + W + T)
        q = (
            q0_ref[at].astype(F32) + q1_ref[at].astype(F32)
            + q2_ref[at].astype(F32) + q3_ref[at].astype(F32)
        ).astype(BF)
        g = g_ref[at]
        k = k_ref[window]
        v = v_ref[window]
        s = mm(q, k, ((1,), (1,)))
        sa, sb, sc = s[:, :T], s[:, T : 2 * T], s[:, 2 * T :]
        if i < 2:
            sa = jnp.where(inside, sa, -1e30)
        if i < 1:
            sb = jnp.where(inside, sb, -1e30)
        sm = jnp.where(old, sa, sc)
        top = jnp.max(jnp.maximum(sm, sb), axis=1, keepdims=True)
        em = jnp.exp2((sm - top) * (SCALE * LOG2E))
        eb = jnp.exp2((sb - top) * (SCALE * LOG2E))
        inv = 1.0 / jnp.sum(em + eb, axis=1, keepdims=True)
        pm = em * inv
        pb = eb * inv
        prob = jnp.concatenate(
            [
                jnp.where(old, pm, 0.0).astype(BF),
                pb.astype(BF),
                jnp.where(old, 0.0, pm).astype(BF),
            ],
            axis=1,
        )
        o_ref[at] = mm(prob, v, ((1,), (0,))).astype(BF)
        dp = mm(g, v, ((1,), (1,)))
        dpm = jnp.where(old, dp[:, :T], dp[:, 2 * T :])
        dpb = dp[:, T : 2 * T]
        delta = jnp.sum(pm * dpm + pb * dpb, axis=1, keepdims=True)
        dsm = pm * (dpm - delta) * SCALE
        dsb = pb * (dpb - delta) * SCALE
        ds = jnp.concatenate(
            [
                jnp.where(old, dsm, 0.0).astype(BF),
                dsb.astype(BF),
                jnp.where(old, 0.0, dsm).astype(BF),
            ],
            axis=1,
        )
        dq_ref[at] = mm(ds, k, ((1,), (0,))).astype(BF)
        dk_ref[window] += mm(ds, q, ((0,), (0,)))
        dv_ref[window] += mm(prob, g, ((0,), (0,)))
    for half in range(2):
        dprev_ref[half, 0] = dk_ref[half * T : (half + 1) * T].astype(BF)
        dprev_ref[half, 1] = dv_ref[half * T : (half + 1) * T].astype(BF)
    for k, row in enumerate(tokens):
        out_ref[k] = o_ref[pl.ds(row, T), :]
        dkv_ref[k, 0] = dk_ref[pl.ds(W + row, T), :]
        dkv_ref[k, 1] = dv_ref[pl.ds(W + row, T), :]


def attend(place, parts, pieces, prev):
    vm = pl.BlockSpec(memory_space=pltpu.VMEM)
    n = 4 * T
    return pl.pallas_call(
        attend_kernel,
        in_specs=[pl.BlockSpec(memory_space=pltpu.SMEM)] + [vm] * 9,
        out_specs=[vm] * 4,
        out_shape=[
            jax.ShapeDtypeStruct((4, T, DH), BF),
            jax.ShapeDtypeStruct((n, DH), BF),
            jax.ShapeDtypeStruct((4, 2, T, DH), F32),
            jax.ShapeDtypeStruct((2, 2, T, DH), BF),
        ],
        scratch_shapes=[
            pltpu.VMEM((W + n, DH), BF),
            pltpu.VMEM((W + n, DH), BF),
            pltpu.VMEM((n, DH), BF),
            pltpu.VMEM((n, DH), BF),
            pltpu.VMEM((W + n, DH), F32),
            pltpu.VMEM((W + n, DH), F32),
        ],
        compiler_params=params(20),
        cost_estimate=cost(12 * n * 768 * DH, 5 << 20, n * W),
        name="attend",
    )(place, *parts, *pieces, *prev)


def tie(*groups):
    flat = iter(lax.optimization_barrier([a for group in groups for a in group]))
    return [[next(flat) for _ in group] for group in groups]


def after(group, *others):
    return tie(group, others)[0]


def per_device(hidden, weight, keys, values, d_attended):
    z, yl, co, yh, x = (lax.axis_index(a) for a in AXES)
    quad = [(a, b) for a in range(2) for b in range(2)]
    blocks = [(yh ^ dy) * NX + (x - dx) % NX for dx in range(NX) for dy in range(2)]
    rows = [(yl ^ dl) * 2 + (co ^ dc) for dc, dl in quad]
    heads = [(yl ^ dl) * 2 + (co ^ dc) for dl, dc in quad]
    lanes = [(yl ^ dl) * 4 + (yh ^ dy) for dy, dl in quad]
    tail = heads + lanes + [yh, 1 - yh, (z % SEQ_Z == 0).astype(jnp.int32)]
    place = jnp.stack(blocks + rows + tail).astype(jnp.int32)

    def weight_piece(dc, dy):
        half = lax.dynamic_slice_in_dim(weight, (yh ^ dy) * DH, DH, 0)
        return jnp.concatenate(
            [
                lax.dynamic_slice_in_dim(half, ((yl ^ dl) * 2 + (co ^ dc)) * DH, DH, 1)
                for dl in range(2)
            ],
            axis=1,
        )

    kvd = [
        jnp.stack(
            [lax.dynamic_slice_in_dim(a, heads[k] * DH, DH, 1) for a in (keys, values, d_attended)]
        )
        for k in range(4)
    ]

    sent = [weight_piece(dc, dy) for dc, dy in quad]
    got = [sent[0], move(sent[1], yh=1), move(sent[2], co=1), move(sent[3], co=1, yh=1)]
    mine = jnp.concatenate(got[:2], axis=1)
    theirs = jnp.concatenate(got[2:], axis=1)
    shard = jnp.concatenate(
        [jnp.where(co == 0, mine, theirs), jnp.where(co == 0, theirs, mine)], axis=0
    )

    def hidden_piece(dy, dl):
        part = lax.dynamic_slice_in_dim(hidden, (yl ^ dl) * 2 * T, 2 * T, 1)
        part = part.reshape(T, 2, 2, DH)
        return lax.dynamic_index_in_dim(part, yh ^ dy, 2, keepdims=False).reshape(T, T)

    mixed = [hidden_piece(dy, dl) for dy, dl in quad]
    mixed = [mixed[0]] + [move(mixed[k], yh=quad[k][0], yl=quad[k][1]) for k in (1, 2, 3)]
    mixed = jnp.stack(mixed).reshape(2, 2, T, T)

    own = [move(mixed, dx=dx) if dx else mixed for dx in range(NX)]
    other = [move(block, co=1) for block in own]
    kvd = after(kvd, mixed)
    swapped = move(jnp.stack([kvd[1], kvd[3]]), co=1)
    pieces = [kvd[0], swapped, move(jnp.stack([kvd[2], swapped[1]]), yl=1)]
    weights = lax.all_gather(shard, "z", axis=0, tiled=False)
    own, other, (weights,) = tie(own, other, (weights,))

    parts = query_part(place, own, other, weights)
    pieces = after(pieces, *parts)
    low = jnp.where(yl == 1, jnp.stack([pieces[0][:2], pieces[1][0, :2]]), pieces[2][:, :2])
    prev = [move(lax.dynamic_index_in_dim(low, co ^ k, 0, keepdims=False), dz=1) for k in range(2)]
    parts = [parts[0]] + [move(parts[k], yh=k // 2, yl=k % 2) for k in (3, 2, 1)]
    attended, dq, dkv, dprev = attend(place, parts, pieces, prev)
    dq = [dq] + [move(dq, yh=k // 2, yl=k % 2) for k in range(1, 4)]

    late = [move(dprev[half], dz=-1) for half in range(2)]
    dq, late = tie(dq, late)
    late = jnp.stack(late)

    sums, away = d_weight_part(place, own, other, dq, weights)
    shard = lax.psum_scatter(sums.reshape(NZ * T, 4 * DH), "z", scatter_dimension=0, tiled=True)
    away = move(away, co=1)
    near = d_hidden_near(place, dq, weights, away)
    line = [near[0]] + [move(near[dx], dx=-dx) for dx in range(1, NX)]

    outs = []
    for k, (dl, dc) in enumerate(quad):
        half = lax.dynamic_index_in_dim(late, co ^ dc, 0, keepdims=False).astype(F32)
        grads = dkv[k] + jnp.where((yl ^ dl) == 1, half, 0.0)
        outs.append(jnp.concatenate([attended[k][None], grads.astype(BF)], axis=0))

    crossed = move(jnp.stack(outs[2:]), yl=1)
    outs = [outs[0], move(jnp.stack([outs[1], crossed[1]]), co=1), crossed]
    result = in_vmem(
        attended_kernel, "attended_last", cost(0, 1 << 20), [((T, 4 * DH), BF)] * 3, place, *outs
    )

    def weight_back(dc, dy):
        block = lax.dynamic_slice_in_dim(shard, (co ^ dc) * DH, DH, 0)
        return block[:, dy * T : (dy + 1) * T]

    ends = [weight_back(dc, dy) for dy, dc in quad]
    ends = [move(ends[k], yh=quad[k][0], co=quad[k][1]) if k else ends[0] for k in range(4)]
    line = sum(block.astype(F32) for block in line).astype(BF)
    back = [line[dy, dl] for dy, dl in quad]
    back = [back[0]] + [move(back[k], yh=quad[k][0], yl=quad[k][1]) for k in (1, 2, 3)]
    back += ends
    d_hidden, d_weight = in_vmem(
        last_kernel, "last", cost(0, 1 << 20), [((T, 8 * DH), BF), ((T, 4 * DH), BF)], place, *back
    )

    return result[0], d_hidden, d_weight, result[1], result[2]


def solution(mesh):
    grid = Mesh(mesh.devices.reshape(SIZES), AXES)
    spec = P(("z", "yl", "co"), ("yh", "x"))
    return jax.shard_map(
        per_device, mesh=grid, in_specs=(spec,) * 5, out_specs=(spec,) * 5, check_vma=False
    )
```

```python
import jax
import jax.numpy as jnp
from jax import lax
from jax.experimental import pallas as pl
from jax.experimental.pallas import tpu as pltpu
from jax.sharding import Mesh, PartitionSpec as P

DH = 128
W = 512
SEQ_Z = 4
AXES = ("z", "yl", "co", "yh", "x")
SIZES = (8, 2, 2, 2, 4)
NZ, NX = 8, 4
T = 256
SCALE = 1.0 / DH**0.5
LOG2E = 1.4426950408889634
BF = jnp.bfloat16
F32 = jnp.float32


def route(target):
    pairs = []
    for i in range(256):
        rest, place = i, []
        for size in SIZES[::-1]:
            place.append(rest % size)
            rest //= size
        there = target(*place[::-1])
        j = 0
        for size, c in zip(SIZES, there):
            j = j * size + c % size
        pairs.append((i, j))
    return pairs


def move(block, dz=0, yl=0, co=0, yh=0, dx=0):
    pairs = route(lambda z, a, b, c, x: (z + dz, a ^ yl, b ^ co, c ^ yh, x + dx))
    return lax.ppermute(block, AXES, pairs)


def params(mebibytes=20):
    return pltpu.CompilerParams(vmem_limit_bytes=mebibytes * 1024 * 1024)


def cost(flops, bytes_accessed, exps=0):
    return pl.CostEstimate(flops=flops, bytes_accessed=bytes_accessed, transcendentals=exps)


def mm(a, b, dims):
    return lax.dot_general(a, b, (dims, ((), ())), preferred_element_type=F32)


def feature_block(tokens, i, dl):
    return tokens[i // 2][i % 2, dl]


def query_kernel(place_ref, *refs):
    own, other, w_ref, outs = refs[:4], refs[4:8], refs[8], refs[9:13]
    w = jnp.concatenate([w_ref[place_ref[i]] for i in range(8)], axis=0)
    for dc, tokens in enumerate((own, other)):
        for dl in range(2):
            h = jnp.concatenate([feature_block(tokens, i, dl) for i in range(8)], axis=1)
            part = mm(h, w, ((1,), (0,))).astype(BF)
            row = pl.multiple_of(place_ref[8 + dc * 2 + dl] * T, T)
            for k in range(4):
                outs[k][pl.ds(row, T), :] = part[:, k * DH : (k + 1) * DH]


def in_vmem(kernel, name, work, outs, *args, room=20):
    vm = pl.BlockSpec(memory_space=pltpu.VMEM)
    return pl.pallas_call(
        kernel,
        in_specs=[pl.BlockSpec(memory_space=pltpu.SMEM)] + [vm] * (len(args) - 1),
        out_specs=[vm] * len(outs),
        out_shape=[jax.ShapeDtypeStruct(shape, kind) for shape, kind in outs],
        compiler_params=params(room),
        cost_estimate=work,
        name=name,
    )(*args)


def query_part(place, own, other, weights):
    work = cost(2 * 1024 * 2048 * 512, 7 << 20)
    outs = [((4 * T, DH), BF)] * 4
    return in_vmem(query_kernel, "query_part", work, outs, place, *own, *other, weights, room=20)


def d_hidden_block(place_ref, refs, dl, i):
    row = pl.multiple_of(place_ref[8 + dl] * T, T)
    dq = jnp.concatenate([refs[k][pl.ds(row, T), :] for k in range(4)], axis=1)
    return mm(dq, refs[4][place_ref[i]], ((1,), (1,)))


def d_hidden_near_kernel(place_ref, *refs):
    for dl in range(2):
        for i in range(8):
            part = d_hidden_block(place_ref, refs, dl, i)
            refs[6 + i // 2][i % 2, dl] = (part + refs[5][i, dl].astype(F32)).astype(BF)


def d_hidden_near(place, dq, weights, away):
    work = cost(1024 * 2048 * 512, 7 << 20)
    outs = [((2, 2, T, T), BF)] * 4
    return in_vmem(d_hidden_near_kernel, "d_hidden_near", work, outs, place, *dq, weights, away, room=40)


def d_weight_kernel(place_ref, *refs):
    own, other, dqs, out_ref, away_ref = refs[:4], refs[4:8], refs[8:12], refs[13], refs[14]
    dq = jnp.concatenate(
        [
            jnp.concatenate(
                [
                    ref[pl.ds(pl.multiple_of(place_ref[8 + j] * T, T), T), :]
                    for ref in dqs
                ],
                axis=1,
            )
            for j in range(4)
        ],
        axis=0,
    )
    for i in range(8):
        h = jnp.concatenate(
            [feature_block(tokens, i, dl) for tokens in (own, other) for dl in range(2)], axis=0
        )
        out_ref[place_ref[i]] = mm(h, dq, ((0,), (0,))).astype(BF)
    for dl in range(2):
        for i in range(8):
            away_ref[i, dl] = d_hidden_block(place_ref, refs[8:13], dl + 2, i).astype(BF)


def d_weight_part(place, own, other, dq, weights):
    work = cost(3 * 1024 * 2048 * 512, 11 << 20)
    outs = [((NZ, T, 4 * DH), BF), ((8, 2, T, T), BF)]
    return in_vmem(
        d_weight_kernel, "d_weight_part", work, outs, place, *own, *other, *dq, weights
    )


def attended_kernel(place_ref, own_ref, core_ref, y_ref, *outs):
    for k, ref in enumerate((own_ref, core_ref.at[0], y_ref.at[0], core_ref.at[1])):
        at = pl.multiple_of(place_ref[12 + k] * DH, DH)
        for j in range(3):
            outs[j][:, pl.ds(at, DH)] = ref[j]


def last_kernel(place_ref, *refs):
    for k in range(4):
        at = place_ref[16 + k]
        for co in range(2):
            first = pl.multiple_of((at + co * 2) * DH, DH)
            refs[8][:, pl.ds(first, DH)] = refs[k][:, co * DH : (co + 1) * DH]
    for dy in range(2):
        row = pl.multiple_of(place_ref[20 + dy] * DH, DH)
        for dc in range(2):
            for dl in range(2):
                at = pl.multiple_of(place_ref[12 + dl * 2 + dc] * DH, DH)
                refs[9][pl.ds(row, DH), pl.ds(at, DH)] = refs[4 + dy * 2 + dc][
                    :, dl * DH : (dl + 1) * DH
                ]


def attend_kernel(
    place_ref, q0_ref, q1_ref, q2_ref, q3_ref, p0_ref, p1_ref, p2_ref, prev0_ref, prev1_ref,
    out_ref, dq_ref, dkv_ref, dprev_ref, k_ref, v_ref, g_ref, o_ref, dk_ref, dv_ref,
):
    tokens = [pl.multiple_of(place_ref[12 + k] * T, T) for k in range(4)]
    for half, ref in enumerate((prev0_ref, prev1_ref)):
        k_ref[half * T : (half + 1) * T] = ref[0]
        v_ref[half * T : (half + 1) * T] = ref[1]
    for row, ref in zip(tokens, (p0_ref, p1_ref.at[0], p2_ref.at[0], p2_ref.at[1])):
        k_ref[pl.ds(W + row, T), :] = ref[0]
        v_ref[pl.ds(W + row, T), :] = ref[1]
        g_ref[pl.ds(row, T), :] = ref[2]
    dk_ref[...] = jnp.zeros_like(dk_ref)
    dv_ref[...] = jnp.zeros_like(dv_ref)
    inside = place_ref[22] == 0
    rows = lax.broadcasted_iota(jnp.int32, (T, T), 0)
    cols = lax.broadcasted_iota(jnp.int32, (T, T), 1)
    old = cols > rows
    for i in range(4):
        at = slice(i * T, (i + 1) * T)
        window = slice(i * T, i * T + W + T)
        q = (
            q0_ref[at].astype(F32) + q1_ref[at].astype(F32)
            + q2_ref[at].astype(F32) + q3_ref[at].astype(F32)
        ).astype(BF)
        g = g_ref[at]
        k = k_ref[window]
        v = v_ref[window]
        s = mm(q, k, ((1,), (1,)))
        sa, sb, sc = s[:, :T], s[:, T : 2 * T], s[:, 2 * T :]
        if i < 2:
            sa = jnp.where(inside, sa, -1e30)
        if i < 1:
            sb = jnp.where(inside, sb, -1e30)
        sm = jnp.where(old, sa, sc)
        top = jnp.max(jnp.maximum(sm, sb), axis=1, keepdims=True)
        em = jnp.exp2((sm - top) * (SCALE * LOG2E))
        eb = jnp.exp2((sb - top) * (SCALE * LOG2E))
        inv = 1.0 / jnp.sum(em + eb, axis=1, keepdims=True)
        pm = em * inv
        pb = eb * inv
        prob = jnp.concatenate(
            [
                jnp.where(old, pm, 0.0).astype(BF),
                pb.astype(BF),
                jnp.where(old, 0.0, pm).astype(BF),
            ],
            axis=1,
        )
        o_ref[at] = mm(prob, v, ((1,), (0,))).astype(BF)
        dp = mm(g, v, ((1,), (1,)))
        dpm = jnp.where(old, dp[:, :T], dp[:, 2 * T :])
        dpb = dp[:, T : 2 * T]
        delta = jnp.sum(pm * dpm + pb * dpb, axis=1, keepdims=True)
        dsm = pm * (dpm - delta) * SCALE
        dsb = pb * (dpb - delta) * SCALE
        ds = jnp.concatenate(
            [
                jnp.where(old, dsm, 0.0).astype(BF),
                dsb.astype(BF),
                jnp.where(old, 0.0, dsm).astype(BF),
            ],
            axis=1,
        )
        dq_ref[at] = mm(ds, k, ((1,), (0,))).astype(BF)
        dk_ref[window] += mm(ds, q, ((0,), (0,)))
        dv_ref[window] += mm(prob, g, ((0,), (0,)))
    for half in range(2):
        dprev_ref[half, 0] = dk_ref[half * T : (half + 1) * T].astype(BF)
        dprev_ref[half, 1] = dv_ref[half * T : (half + 1) * T].astype(BF)
    for k, row in enumerate(tokens):
        out_ref[k] = o_ref[pl.ds(row, T), :]
        dkv_ref[k, 0] = dk_ref[pl.ds(W + row, T), :]
        dkv_ref[k, 1] = dv_ref[pl.ds(W + row, T), :]


def attend(place, parts, pieces, prev):
    vm = pl.BlockSpec(memory_space=pltpu.VMEM)
    n = 4 * T
    return pl.pallas_call(
        attend_kernel,
        in_specs=[pl.BlockSpec(memory_space=pltpu.SMEM)] + [vm] * 9,
        out_specs=[vm] * 4,
        out_shape=[
            jax.ShapeDtypeStruct((4, T, DH), BF),
            jax.ShapeDtypeStruct((n, DH), BF),
            jax.ShapeDtypeStruct((4, 2, T, DH), F32),
            jax.ShapeDtypeStruct((2, 2, T, DH), BF),
        ],
        scratch_shapes=[
            pltpu.VMEM((W + n, DH), BF),
            pltpu.VMEM((W + n, DH), BF),
            pltpu.VMEM((n, DH), BF),
            pltpu.VMEM((n, DH), BF),
            pltpu.VMEM((W + n, DH), F32),
            pltpu.VMEM((W + n, DH), F32),
        ],
        compiler_params=params(20),
        cost_estimate=cost(12 * n * 768 * DH, 5 << 20, n * W),
        name="attend",
    )(place, *parts, *pieces, *prev)


def tie(*groups):
    flat = iter(lax.optimization_barrier([a for group in groups for a in group]))
    return [[next(flat) for _ in group] for group in groups]


def after(group, *others):
    return tie(group, others)[0]


def per_device(hidden, weight, keys, values, d_attended):
    z, yl, co, yh, x = (lax.axis_index(a) for a in AXES)
    quad = [(a, b) for a in range(2) for b in range(2)]
    blocks = [(yh ^ dy) * NX + (x - dx) % NX for dx in range(NX) for dy in range(2)]
    rows = [(yl ^ dl) * 2 + (co ^ dc) for dc, dl in quad]
    heads = [(yl ^ dl) * 2 + (co ^ dc) for dl, dc in quad]
    lanes = [(yl ^ dl) * 4 + (yh ^ dy) for dy, dl in quad]
    tail = heads + lanes + [yh, 1 - yh, (z % SEQ_Z == 0).astype(jnp.int32)]
    place = jnp.stack(blocks + rows + tail).astype(jnp.int32)

    def weight_piece(dc, dy):
        half = lax.dynamic_slice_in_dim(weight, (yh ^ dy) * DH, DH, 0)
        return jnp.concatenate(
            [
                lax.dynamic_slice_in_dim(half, ((yl ^ dl) * 2 + (co ^ dc)) * DH, DH, 1)
                for dl in range(2)
            ],
            axis=1,
        )

    kvd = [
        jnp.stack(
            [lax.dynamic_slice_in_dim(a, heads[k] * DH, DH, 1) for a in (keys, values, d_attended)]
        )
        for k in range(4)
    ]

    sent = [weight_piece(dc, dy) for dc, dy in quad]
    got = [sent[0], move(sent[1], yh=1), move(sent[2], co=1), move(sent[3], co=1, yh=1)]
    mine = jnp.concatenate(got[:2], axis=1)
    theirs = jnp.concatenate(got[2:], axis=1)
    shard = jnp.concatenate(
        [jnp.where(co == 0, mine, theirs), jnp.where(co == 0, theirs, mine)], axis=0
    )

    def hidden_piece(dy, dl):
        part = lax.dynamic_slice_in_dim(hidden, (yl ^ dl) * 2 * T, 2 * T, 1)
        part = part.reshape(T, 2, 2, DH)
        return lax.dynamic_index_in_dim(part, yh ^ dy, 2, keepdims=False).reshape(T, T)

    mixed = [hidden_piece(dy, dl) for dy, dl in quad]
    mixed = [mixed[0]] + [move(mixed[k], yh=quad[k][0], yl=quad[k][1]) for k in (1, 2, 3)]
    mixed = jnp.stack(mixed).reshape(2, 2, T, T)

    own = [move(mixed, dx=dx) if dx else mixed for dx in range(NX)]
    other = [move(block, co=1) for block in own]
    kvd = after(kvd, mixed)
    swapped = move(jnp.stack([kvd[1], kvd[3]]), co=1)
    pieces = [kvd[0], swapped, move(jnp.stack([kvd[2], swapped[1]]), yl=1)]
    weights = lax.all_gather(shard, "z", axis=0, tiled=False)
    own, other, (weights,) = tie(own, other, (weights,))

    parts = query_part(place, own, other, weights)
    pieces = after(pieces, *parts)
    low = jnp.where(yl == 1, jnp.stack([pieces[0][:2], pieces[1][0, :2]]), pieces[2][:, :2])
    prev = [move(lax.dynamic_index_in_dim(low, co ^ k, 0, keepdims=False), dz=1) for k in range(2)]
    parts = [parts[0]] + [move(parts[k], yh=k // 2, yl=k % 2) for k in (3, 2, 1)]
    attended, dq, dkv, dprev = attend(place, parts, pieces, prev)
    dq = [dq] + [move(dq, yh=k // 2, yl=k % 2) for k in range(1, 4)]

    late = [move(dprev[half], dz=-1) for half in range(2)]
    dq, late = tie(dq, late)
    late = jnp.stack(late)

    sums, away = d_weight_part(place, own, other, dq, weights)
    shard = lax.psum_scatter(sums.reshape(NZ * T, 4 * DH), "z", scatter_dimension=0, tiled=True)
    away = move(away, co=1)
    near = d_hidden_near(place, dq, weights, away)
    line = [near[0]] + [move(near[dx], dx=-dx) for dx in range(1, NX)]

    outs = []
    for k, (dl, dc) in enumerate(quad):
        half = lax.dynamic_index_in_dim(late, co ^ dc, 0, keepdims=False).astype(F32)
        grads = dkv[k] + jnp.where((yl ^ dl) == 1, half, 0.0)
        outs.append(jnp.concatenate([attended[k][None], grads.astype(BF)], axis=0))

    crossed = move(jnp.stack(outs[2:]), yl=1)
    outs = [outs[0], move(jnp.stack([outs[1], crossed[1]]), co=1), crossed]
    result = in_vmem(
        attended_kernel, "attended_last", cost(0, 1 << 20), [((T, 4 * DH), BF)] * 3, place, *outs
    )

    def weight_back(dc, dy):
        block = lax.dynamic_slice_in_dim(shard, (co ^ dc) * DH, DH, 0)
        return block[:, dy * T : (dy + 1) * T]

    ends = [weight_back(dc, dy) for dy, dc in quad]
    ends = [move(ends[k], yh=quad[k][0], co=quad[k][1]) if k else ends[0] for k in range(4)]
    line = sum(block.astype(F32) for block in line).astype(BF)
    back = [line[dy, dl] for dy, dl in quad]
    back = [back[0]] + [move(back[k], yh=quad[k][0], yl=quad[k][1]) for k in (1, 2, 3)]
    back += ends
    d_hidden, d_weight = in_vmem(
        last_kernel, "last", cost(0, 1 << 20), [((T, 8 * DH), BF), ((T, 4 * DH), BF)], place, *back
    )

    return result[0], d_hidden, d_weight, result[1], result[2]


def solution(mesh):
    grid = Mesh(mesh.devices.reshape(SIZES), AXES)
    spec = P(("z", "yl", "co"), ("yh", "x"))
    return jax.shard_map(
        per_device, mesh=grid, in_specs=(spec,) * 5, out_specs=(spec,) * 5, check_vma=False
    )
```
